256 devices in a mesh: seq: 16 (over z_hi, y, core), chan: 16 (over x, z_lo).
Axes of the slice: x: 4, y: 4, z: 8 (z_hi: 2, z_lo: 4; z = z_hi * 4 + z_lo), core: 2. Of those that a mesh axis runs over, the one named last changes fastest.
Arguments:
- query: bfloat16 [4096, 8192], P('seq', 'chan'), may hold values from -6 to 6
- key_in: bfloat16 [4096, 8192], P('seq', 'chan'), may hold values from -6 to 6
- value_in: bfloat16 [4096, 8192], P('seq', 'chan'), may hold values from -6 to 6
- filter_taps: float32 [4096, 8192], P('seq', 'chan'), may hold values from -4 to 4
- conv_bias: float32 [8192], P('chan'), may hold values from -4 to 4
- out_weight: bfloat16 [8192, 8192], P('seq', 'chan'), may hold values from -0.0625 to 0.0625
Outputs:
- block_out: bfloat16 [4096, 8192], P('seq', 'chan')
The draws below stay inside these ranges and needn't reach their ends.
All inputs are finite; a program needn't handle non-finite values.
Results may differ from the reference program's by a relative error of at most 0.0049.
Values may be sent and summed in bfloat16 or wider, within the bound.
No kernel may reach another device: no remote copies, remote signals or barrier semaphores. Data moves between devices by JAX's collectives and lax.ppermute only.
A program may use at most 64 MiB of HBM per device.

```python
import math
import jax
import jax.numpy as jnp
from jax import lax

D = 8192
TOK_DEV = 256
SEQUENCE_LENGTH = 4096


def draw_filter_taps(key, part):
    key = jax.random.fold_in(key, 7)
    sub_keys = jax.random.split(key, 8)
    length = SEQUENCE_LENGTH
    slow_share = 0.5
    noisy_component = jnp.clip(jax.random.normal(sub_keys[0], (SEQUENCE_LENGTH, D), jnp.float32), -4.0, 4.0)
    chooser = jax.random.uniform(sub_keys[1], (D,), jnp.float32)
    is_fast = chooser >= slow_share
    slow_rate = jax.random.uniform(sub_keys[2], (D,), jnp.float32, 0.05, 0.3) * (math.log(10.0) / length)
    fast_rate = 1.0 / jax.random.uniform(sub_keys[3], (D,), jnp.float32, 30.0, 50.0)
    falloff_speed = jnp.where(is_fast, fast_rate, slow_rate)
    tap_positions = jax.random.randint(sub_keys[4], (2, D), 1, SEQUENCE_LENGTH)
    falloff_factor = jax.random.uniform(sub_keys[5], (2, D), jnp.float32, 0.5, 0.8)
    leading_reflection = jax.random.randint(sub_keys[6], (D,), TOK_DEV, 2 * TOK_DEV)
    reflection_spacing = jax.random.randint(sub_keys[7], (D,), TOK_DEV // 2, TOK_DEV + 1)
    lag_dimension = jnp.arange(SEQUENCE_LENGTH, dtype=jnp.int32)[:, None]
    after_echo = lag_dimension - leading_reflection[None, :]
    since_fast = jnp.where(after_echo < 0, lag_dimension, jnp.remainder(jnp.maximum(after_echo, 0), reflection_spacing[None, :]))
    since_start = jnp.where(is_fast[None, :], since_fast, lag_dimension)
    spike_amplitude = jnp.where(lag_dimension >= tap_positions[0][None, :], falloff_factor[0][None, :], 1.0)
    spike_amplitude = spike_amplitude * jnp.where(lag_dimension >= tap_positions[1][None, :], falloff_factor[1][None, :], 1.0)
    decay_envelope = jnp.exp(-falloff_speed[None, :] * since_start.astype(jnp.float32))
    impulse_number = (2 + (SEQUENCE_LENGTH - 1 - leading_reflection) // reflection_spacing).astype(jnp.float32)
    slow_energy = (1.0 - jnp.exp(-2.0 * falloff_speed * length)) / (1.0 - jnp.exp(-2.0 * falloff_speed))
    fast_falloff_power = impulse_number / (1.0 - jnp.exp(-2.0 * falloff_speed))
    resulting_taps = jnp.where(is_fast, fast_falloff_power, slow_energy)
    return (decay_envelope * spike_amplitude * noisy_component / jnp.sqrt(resulting_taps)[None, :]).astype(jnp.float32)


def block_scale(rng, extent, pieces, least, largest):
    factor_of = 1.0
    for dim, blocks in pieces:
        heights = jax.random.uniform(jax.random.fold_in(jax.random.fold_in(rng, 6), dim), (blocks,), jnp.float32, least / len(pieces), largest / len(pieces))
        factor_of = factor_of * jnp.repeat(jnp.exp(heights), extent[dim] // blocks).reshape((-1,) + (1,) * (len(extent) - 1 - dim))
    return factor_of


def gaussian(own_key, shape, spread, most, pieces=(), kind=jnp.bfloat16):
    drawn = jax.random.normal(own_key, shape, jnp.float32) * spread
    if len(pieces) > 0:
        drawn = block_scale(own_key, shape, pieces, -0.22, 0.18) * drawn
    return jnp.clip(drawn, min=-most, max=most).astype(kind)


def setup_inputs(seed: int = 0) -> dict:
    seeds = jax.random.split(jax.random.key(seed), 7)
    query = gaussian(seeds[0], (SEQUENCE_LENGTH, D), 1.0, 6.0, ((0, 16), (1, 16)))
    key_in = gaussian(seeds[1], (SEQUENCE_LENGTH, D), 1.0, 6.0, ((0, 16), (1, 16)))
    value_in = gaussian(seeds[2], (SEQUENCE_LENGTH, D), 1.0, 6.0, ((0, 16), (1, 16)))
    filter_taps = draw_filter_taps(jax.random.fold_in(seeds[6], 71), 0)
    conv_bias = gaussian(seeds[4], (D,), 1.0, 4.0, ((0, 16),), jnp.float32)
    out_weight = gaussian(seeds[5], (D, D), D ** -0.5, 0.0625, ((0, 16), (1, 16)))
    return {"query": query, "key_in": key_in, "value_in": value_in, "filter_taps": filter_taps, "conv_bias": conv_bias, "out_weight": out_weight}


def reference(query, key_in, value_in, filter_taps, conv_bias, out_weight):
    signal_in = key_in.astype(jnp.float32) * value_in.astype(jnp.float32)
    group_width = math.gcd(D, 512)
    groups = D // group_width

    def by_group(array_in):
        return array_in.reshape(SEQUENCE_LENGTH, groups, group_width).transpose(1, 0, 2)

    def convolve(operands):
        signal, filter_part = operands
        fft_size = 2 * SEQUENCE_LENGTH
        spectrum = jnp.fft.rfft(signal, n=fft_size, axis=0) * jnp.fft.rfft(filter_part, n=fft_size, axis=0)
        return jnp.fft.irfft(spectrum, n=fft_size, axis=0)[:SEQUENCE_LENGTH]

    convolved = lax.map(convolve, (by_group(signal_in), by_group(filter_taps)))
    convolved = convolved.transpose(1, 0, 2).reshape(SEQUENCE_LENGTH, D)
    gated_out = (query.astype(jnp.float32) * (convolved + conv_bias[None, :] * signal_in)).astype(jnp.bfloat16)
    return jnp.dot(gated_out, out_weight, preferred_element_type=jnp.float32).astype(jnp.bfloat16)
```

```python
import functools

import jax
import jax.numpy as jnp
import numpy as np
from jax import lax
from jax.experimental import pallas as pl
from jax.experimental.pallas import tpu as pltpu
from jax.sharding import Mesh
from jax.sharding import PartitionSpec as P

bf16 = jnp.bfloat16
f32 = jnp.float32
AXES = ("h", "y", "k", "x", "l")
SEQ = ("h", "y", "k")
CHAN = ("x", "l")
N = 1024
STEPS = 4
FREQS = 128
MIB = 1 << 20


def transform_tables():
    k = np.arange(N // 2)[:, None]
    a = np.arange(N // 2)[None, :]
    angle = 2.0 * np.pi * ((k * a) % N) / N
    re, im = np.cos(angle), -np.sin(angle)
    im[0] = 1.0 - 2.0 * (np.arange(N // 2) % 2)
    weight = np.full((N // 2, 1), 2.0 / N)
    weight[0] = 1.0 / N
    forward = np.concatenate([re.reshape(STEPS, FREQS, -1), im.reshape(STEPS, FREQS, -1)], 1)
    back = np.concatenate(
        [(re * weight).reshape(STEPS, FREQS, -1), (im * weight).reshape(STEPS, FREQS, -1)], 1
    ).transpose(0, 2, 1)

    def split(m):
        high = m.astype(np.float32).astype(jnp.bfloat16)
        low = (m - high.astype(np.float64)).astype(np.float32).astype(jnp.bfloat16)
        return np.stack([high, low], 1)

    return split(forward), split(back)


def lanes(rows):
    return lax.broadcasted_iota(jnp.int32, (rows, 128), 1)


def swap_groups(blocks):
    a0, a1, a2, a3 = blocks
    lane = lanes(a0.shape[0])
    low, even = lane < 64, (lane & 32) == 0
    roll = lambda v, n: pltpu.roll(v, n, 1)
    b0, b2 = jnp.where(low, a0, roll(a2, 64)), jnp.where(low, roll(a0, 64), a2)
    b1, b3 = jnp.where(low, a1, roll(a3, 64)), jnp.where(low, roll(a1, 64), a3)
    c0, c1 = jnp.where(even, b0, roll(b1, 32)), jnp.where(even, roll(b0, 96), b1)
    c2, c3 = jnp.where(even, b2, roll(b3, 32)), jnp.where(even, roll(b2, 96), b3)
    return c0, c1, c2, c3


def pack_kernel(key_ref, value_ref, taps_ref, out_ref):
    for v in range(4):
        cols = slice(v * 128, (v + 1) * 128)
        signal, taps = [], []
        for r in range(4):
            rows = slice(r * 64, (r + 1) * 64)
            signal.append(key_ref[rows, cols].astype(f32) * value_ref[rows, cols].astype(f32))
            taps.append(taps_ref[rows, cols])
        for which, blocks in enumerate((signal, taps)):
            for y, block in enumerate(swap_groups(blocks)):
                out_ref[v % 2, y, v // 2, which] = block.astype(bf16)


def pick(position, choices):
    return jnp.where(
        position == 0,
        choices[0],
        jnp.where(position == 1, choices[1], jnp.where(position == 2, choices[2], choices[3])),
    )


def conv_kernel(in_ref, fwd_ref, back_ref, *refs):
    out_refs, (sig, taps, spec_s, spec_t, prod, acc, spread) = refs[:4], refs[4:]
    step = pl.program_id(0)

    @pl.when(step == 0)
    def _():
        for which, dst in enumerate((sig, taps)):
            for h in range(2):
                for kk in range(2):
                    blocks = [in_ref[h * 8 + y * 2 + kk, which].astype(f32) for y in range(4)]
                    for r, block in enumerate(swap_groups(blocks)):
                        row = kk * 256 + r * 64
                        dst[row : row + 64, h * 128 : (h + 1) * 128] = block.astype(bf16)
        acc[...] = jnp.zeros_like(acc)

    dot = functools.partial(jnp.dot, preferred_element_type=f32)
    spec_s[...] = dot(fwd_ref[0], sig[...]) + dot(fwd_ref[1], sig[...])
    spec_t[...] = dot(fwd_ref[0], taps[...]) + dot(fwd_ref[1], taps[...])

    rows = 8
    position = lanes(rows) // 32
    row_id = lax.broadcasted_iota(jnp.int32, (rows, 128), 0)
    sign = (1 - 2 * (row_id & 1)).astype(f32)
    first_row = row_id == 0

    def rolled(v):
        return [v] + [pltpu.roll(v, 32 * i, 1) for i in (1, 2, 3)]

    def body(i, carry):
        base = pl.multiple_of(i * rows, rows)
        re, im = pl.ds(base, rows), pl.ds(base + FREQS, rows)
        left, right = slice(0, 128), slice(128, 256)
        s = [rolled(spec_s[part, side]) for side in (left, right) for part in (re, im)]
        t = [rolled(spec_t[part, side]) for side in (left, right) for part in (re, im)]
        total = [[None] * 4 for _ in range(2)]

        def add(tile, tap, src):
            terms = (tap[0] * src[0], tap[1] * src[1], tap[1] * src[0], tap[0] * src[1])
            for n, term in enumerate(terms):
                total[tile][n] = term if total[tile][n] is None else total[tile][n] + term

        for j in range(4):
            near = [pick(position, [t[part][(p - j) % 4] for p in range(4)]) for part in (0, 1)]
            far = [pick(position, [t[part][(p - j) % 4] for p in range(4)]) for part in (2, 3)]
            here = position >= j
            shifted = [jnp.where(here, s[part][j], 0.0) for part in (0, 1)]
            mixed = [jnp.where(here, s[part + 2][j], s[part][j]) for part in (0, 1)]
            add(0, near, shifted)
            add(1, near, mixed)
            add(1, far, shifted)
        special = jnp.logical_and(first_row, jnp.logical_and(step == 0, i == 0))
        prods = []
        for rr, ii, ri, ir in total:
            prods.append((rr - jnp.where(special, 0.0, ii), jnp.where(special, ii, ri + ir)))
        for part, dst in enumerate((re, im)):
            p0, p1 = prods[0][part], prods[1][part]
            q0, q1 = pltpu.roll(p0, 32, 1), pltpu.roll(p1, 32, 1)
            prod[dst, left] = p0 + sign * jnp.where(position >= 1, q0, 0.0)
            prod[dst, right] = p1 + sign * jnp.where(position >= 1, q1, q0)
        return carry

    lax.fori_loop(0, FREQS // rows, body, 0, unroll=2)
    whole = prod[...]
    high = whole.astype(bf16)
    low = (whole - high.astype(f32)).astype(bf16)
    acc[...] += dot(back_ref[0], high) + dot(back_ref[1], high) + dot(back_ref[0], low)

    @pl.when(step == STEPS - 1)
    def _():
        my_h, my_y = lax.axis_index("h"), lax.axis_index("y")
        for h in range(2):
            for kk in range(2):
                blocks = [
                    acc[kk * 256 + r * 64 : kk * 256 + (r + 1) * 64, h * 128 : (h + 1) * 128]
                    for r in range(4)
                ]
                for y, block in enumerate(swap_groups(blocks)):
                    spread[h, y, kk] = block.astype(bf16)
        for shift, out_ref in enumerate(out_refs):
            for far in range(2):
                out_ref[far] = spread[(my_h + far) % 2, (my_y + shift) % 4]


def gate_kernel(far, *refs):
    parts, (q0, k0, v0, q1, k1, v1, bias_ref, out_ref, held) = refs[:4], refs[4:]
    my_h, my_y, my_k = lax.axis_index("h"), lax.axis_index("y"), lax.axis_index("k")
    for shift, part in enumerate(parts):
        held[(my_y - shift + 4) % 4] = part[...]
    col = pl.multiple_of((my_k * 2 + (my_h + far) % 2) * 128, 128)
    cols = pl.ds(col, 128)
    bias = bias_ref[:, cols]
    for own, (q, k, v) in enumerate(((q0, k0, v0), (q1, k1, v1))):
        kk = (my_k + own) % 2
        blocks = swap_groups([held[y, kk].astype(f32) for y in range(4)])
        for r, conv in enumerate(blocks):
            rows = slice(r * 64, (r + 1) * 64)
            signal = k[rows, cols].astype(f32) * v[rows, cols].astype(f32)
            out_ref[own, rows, :] = (q[rows, cols].astype(f32) * (conv + bias * signal)).astype(bf16)


def project_kernel(far, last, *refs):
    g, w, rest = refs[:10], refs[10:20], refs[20:]
    if last:
        before, own_ref, other_ref, lhs, rhs, sems = rest
    else:
        out_ref, lhs, rhs, sems = rest
    ax = {a: lax.axis_index(a) for a in AXES}
    half = pl.multiple_of(((ax["h"] + far) % 2) * 128, 128)
    copies = []

    def start(src, dst):
        copy = pltpu.make_async_copy(src, dst, sems.at[len(copies)])
        copy.start()
        copies.append(copy)

    for dh in range(2):
        for which, (dy, parts) in enumerate(((0, (0, 1)), (3, (0, 1)), (1, (0, 1)), (2, (0,)), (2, (1,)))):
            src = w[dh * 5 + which]
            for p in parts:
                h, y, k = (ax["h"] + dh) % 2, (ax["y"] + dy) % 4, (ax["k"] + p) % 2
                row = pl.multiple_of((h * 8 + y * 2 + k) * 128, 128)
                piece = src.at[p] if len(parts) == 2 else src
                start(piece.at[pl.ds(half, 128)], rhs.at[pl.ds(row, 128)])
    for far_l in range(2):
        for which, (dx, parts) in enumerate(((0, (0, 1)), (3, (0, 1)), (1, (0, 1)), (2, (0,)), (2, (1,)))):
            src = g[far_l * 5 + which]
            x = (ax["x"] + dx) % 4
            for p in parts:
                piece = src.at[p] if len(parts) == 2 else src
                rows = pl.ds(p * 256, 256)
                for j in (1, 2, 3) if far_l else (0,):
                    col = pl.multiple_of((x * 4 + (ax["l"] + 4 - j) % 4) * 128, 128)
                    start(piece.at[j - 1] if far_l else piece, lhs.at[rows, pl.ds(col, 128)])
    for copy in copies:
        copy.wait()

    def tile(i, carry):
        rows = pl.ds(pl.multiple_of(i * 128, 128), 128)
        part = jnp.dot(lhs[rows, :], rhs[...], preferred_element_type=f32)
        if last:
            here = pl.ds(pl.multiple_of((i % 2) * 128, 128), 128)

            @pl.when(i < 2)
            def _():
                own_ref[here, :] = before[rows, :] + part

            @pl.when(i >= 2)
            def _():
                other_ref[here, :] = before[rows, :] + part
        else:
            out_ref[rows, :] = part
        return carry

    lax.fori_loop(0, 4, tile, 0)


VMEM = pl.BlockSpec(memory_space=pltpu.VMEM)
ANY = pl.BlockSpec(memory_space=pl.ANY)


def params(limit=48 * MIB, **kw):
    return pltpu.CompilerParams(vmem_limit_bytes=limit, **kw)


def pack(key_in, value_in, taps):
    return pl.pallas_call(
        pack_kernel,
        out_shape=jax.ShapeDtypeStruct((2, 4, 2, 2, 64, 128), bf16),
        in_specs=[VMEM] * 3,
        out_specs=VMEM,
        compiler_params=params(),
        name="pack",
    )(key_in, value_in, taps)


def convolve(received):
    fwd, back = transform_tables()
    out = jax.ShapeDtypeStruct((2, 2, 64, 128), bf16)
    whole = lambda shape: pl.BlockSpec(shape, lambda i: (0,) * len(shape))
    return pl.pallas_call(
        conv_kernel,
        grid=(STEPS,),
        out_shape=[out] * 4,
        in_specs=[
            whole((16, 2, 64, 128)),
            pl.BlockSpec((None, 2, 2 * FREQS, 512), lambda i: (i, 0, 0, 0)),
            pl.BlockSpec((None, 2, 512, 2 * FREQS), lambda i: (i, 0, 0, 0)),
        ],
        out_specs=[whole((2, 2, 64, 128))] * 4,
        scratch_shapes=[
            pltpu.VMEM((512, 256), bf16),
            pltpu.VMEM((512, 256), bf16),
            pltpu.VMEM((2 * FREQS, 256), f32),
            pltpu.VMEM((2 * FREQS, 256), f32),
            pltpu.VMEM((2 * FREQS, 256), f32),
            pltpu.VMEM((512, 256), f32),
            pltpu.VMEM((2, 4, 2, 64, 128), bf16),
        ],
        compiler_params=params(dimension_semantics=("arbitrary",)),
        name="convolve",
    )(received, jnp.asarray(fwd), jnp.asarray(back))


def gate(far, parts, own, partner, bias):
    return pl.pallas_call(
        functools.partial(gate_kernel, far),
        out_shape=jax.ShapeDtypeStruct((2, 256, 128), bf16),
        in_specs=[VMEM] * 11,
        out_specs=VMEM,
        scratch_shapes=[pltpu.VMEM((4, 2, 64, 128), bf16)],
        compiler_params=params(),
        name="gate",
    )(*parts, *own, *partner, bias)


def project(far, gated, weights, before=None):
    last = before is not None
    half = jax.ShapeDtypeStruct((256, 512), f32)
    return pl.pallas_call(
        functools.partial(project_kernel, far, last),
        out_shape=[half] * 2 if last else jax.ShapeDtypeStruct((512, 512), f32),
        in_specs=[ANY] * 20 + [VMEM] * last,
        out_specs=[VMEM] * 2 if last else VMEM,
        scratch_shapes=[
            pltpu.VMEM((512, 2048), bf16),
            pltpu.VMEM((2048, 512), bf16),
            pltpu.SemaphoreType.DMA((48,)),
        ],
        compiler_params=params(),
        name="project",
    )(*gated, *weights, *([before] if last else []))


def shift(v, axis, by):
    n = lax.axis_size(axis)
    return lax.ppermute(v, axis, [(i, (i + by) % n) for i in range(n)])


def ring(v, axis):
    up, down = shift(v, axis, 1), shift(v, axis, -1)
    return [v, up, down, shift(up[0], axis, 1), shift(down[1], axis, -1)]


def gather_gated(v):
    others = jnp.stack([shift(v, "l", j) for j in (1, 2, 3)], axis=1)
    return ring(v, "x") + ring(others, "x")


def body(query, key_in, value_in, filter_taps, conv_bias, out_weight):
    core = lax.axis_index("k")
    packed = pack(key_in, value_in, filter_taps).reshape(16, 2, 64, 128)
    own = (query, key_in, value_in)
    partner = tuple(shift(v, "k", 1) for v in own)
    keep = lax.dynamic_slice(out_weight, (core * 256, 0), (256, 512))
    give = lax.dynamic_slice(out_weight, ((1 - core) * 256, 0), (256, 512))
    weight = jnp.stack([keep, shift(give, "k", 1)])
    weights = ring(weight, "y")
    received = lax.all_to_all(packed, SEQ, split_axis=0, concat_axis=0, tiled=True)
    weights += ring(shift(weight, "h", 1), "y")

    to_y = convolve(received)
    parts = [to_y[0]] + [shift(to_y[s], "y", s) for s in (1, 2, 3)]
    crossing = shift(jnp.stack([p[1] for p in parts]), "h", 1)
    bias = conv_bias.reshape(1, 512)
    near = gather_gated(gate(0, [p[0] for p in parts], own, partner, bias))
    far = gather_gated(gate(1, [crossing[s] for s in range(4)], own, partner, bias))

    half = project(0, near, weights)
    mine, other = project(1, far, weights, half)
    return (mine + shift(other, "k", 1)).astype(bf16)


def solution(mesh):
    fine = Mesh(mesh.devices.reshape(2, 4, 2, 4, 4), AXES)
    block = P(SEQ, CHAN)
    return jax.shard_map(
        body,
        mesh=fine,
        in_specs=(block, block, block, block, P(CHAN), block),
        out_specs=block,
        check_vma=False,
    )
```

```python
import functools

import jax
import jax.numpy as jnp
import numpy as np
from jax import lax
from jax.experimental import pallas as pl
from jax.experimental.pallas import tpu as pltpu
from jax.sharding import Mesh
from jax.sharding import PartitionSpec as P

bf16 = jnp.bfloat16
f32 = jnp.float32
AXES = ("h", "y", "k", "x", "l")
SEQ = ("h", "y", "k")
CHAN = ("x", "l")
N = 1024
STEPS = 4
FREQS = 128
MIB = 1 << 20


def transform_tables():
    k = np.arange(N // 2)[:, None]
    a = np.arange(N // 2)[None, :]
    angle = 2.0 * np.pi * ((k * a) % N) / N
    re, im = np.cos(angle), -np.sin(angle)
    im[0] = 1.0 - 2.0 * (np.arange(N // 2) % 2)
    weight = np.full((N // 2, 1), 2.0 / N)
    weight[0] = 1.0 / N
    forward = np.concatenate([re.reshape(STEPS, FREQS, -1), im.reshape(STEPS, FREQS, -1)], 1)
    back = np.concatenate(
        [(re * weight).reshape(STEPS, FREQS, -1), (im * weight).reshape(STEPS, FREQS, -1)], 1
    ).transpose(0, 2, 1)

    def split(m):
        high = m.astype(np.float32).astype(jnp.bfloat16)
        low = (m - high.astype(np.float64)).astype(np.float32).astype(jnp.bfloat16)
        return np.stack([high, low], 1)

    return split(forward), split(back)


def lanes(rows):
    return lax.broadcasted_iota(jnp.int32, (rows, 128), 1)


def swap_groups(blocks):
    a0, a1, a2, a3 = blocks
    lane = lanes(a0.shape[0])
    low, even = lane < 64, (lane & 32) == 0
    roll = lambda v, n: pltpu.roll(v, n, 1)
    b0, b2 = jnp.where(low, a0, roll(a2, 64)), jnp.where(low, roll(a0, 64), a2)
    b1, b3 = jnp.where(low, a1, roll(a3, 64)), jnp.where(low, roll(a1, 64), a3)
    c0, c1 = jnp.where(even, b0, roll(b1, 32)), jnp.where(even, roll(b0, 96), b1)
    c2, c3 = jnp.where(even, b2, roll(b3, 32)), jnp.where(even, roll(b2, 96), b3)
    return c0, c1, c2, c3


def fetch(pairs, sems):
    copies = [pltpu.make_async_copy(src, dst, sems.at[i]) for i, (src, dst) in enumerate(pairs)]
    for copy in copies:
        copy.start()
    return copies


def pack_kernel(key_hbm, value_hbm, taps_hbm, out_ref, key_ref, value_ref, taps_ref, sems):
    pairs = ((taps_hbm, taps_ref), (key_hbm, key_ref), (value_hbm, value_ref))
    copies = fetch(pairs, sems)

    def scatter(which, read):
        for v in range(4):
            cols = slice(v * 128, (v + 1) * 128)
            blocks = swap_groups([read(slice(r * 64, (r + 1) * 64), cols) for r in range(4)])
            for y, block in enumerate(blocks):
                out_ref[v % 2, y, v // 2, which] = block.astype(bf16)

    copies[0].wait()
    scatter(1, lambda rows, cols: taps_ref[rows, cols])
    copies[1].wait()
    copies[2].wait()
    scatter(0, lambda rows, cols: key_ref[rows, cols].astype(f32) * value_ref[rows, cols].astype(f32))


def pick(position, choices):
    return jnp.where(
        position == 0,
        choices[0],
        jnp.where(position == 1, choices[1], jnp.where(position == 2, choices[2], choices[3])),
    )


def conv_kernel(in_ref, fwd_hbm, back_hbm, *refs):
    out_refs, (fwd, back, both, spec, prod, acc, spread, sems) = refs[:4], refs[4:]
    tables = []
    for i in range(STEPS):
        tables += [(fwd_hbm.at[i], fwd.at[i]), (back_hbm.at[i], back.at[i])]
    copies = fetch(tables, sems)
    for which in range(2):
        for h in range(2):
            for kk in range(2):
                blocks = [in_ref[h * 8 + y * 2 + kk, which].astype(f32) for y in range(4)]
                for r, block in enumerate(swap_groups(blocks)):
                    row, col = kk * 256 + r * 64, which * 256 + h * 128
                    both[row : row + 64, col : col + 128] = block.astype(bf16)

    dot = functools.partial(jnp.dot, preferred_element_type=f32)
    rows = 8
    position = lanes(rows) // 32
    row_id = lax.broadcasted_iota(jnp.int32, (rows, 128), 0)
    sign = (1 - 2 * (row_id & 1)).astype(f32)
    first_row = row_id == 0

    def rolled(v):
        return [v] + [pltpu.roll(v, 32 * i, 1) for i in (1, 2, 3)]

    for step in range(STEPS):
        copies[2 * step].wait()
        spec[...] = dot(fwd[step, 0], both[...]) + dot(fwd[step, 1], both[...])

        def body(i, carry, step=step):
            base = pl.multiple_of(i * rows, rows)
            re, im = pl.ds(base, rows), pl.ds(base + FREQS, rows)
            left, right = slice(0, 128), slice(128, 256)
            s = [rolled(spec[part, side]) for side in (left, right) for part in (re, im)]
            left_t, right_t = slice(256, 384), slice(384, 512)
            t = [rolled(spec[part, side]) for side in (left_t, right_t) for part in (re, im)]
            total = [[None] * 4 for _ in range(2)]

            def add(tile, tap, src):
                terms = (tap[0] * src[0], tap[1] * src[1], tap[1] * src[0], tap[0] * src[1])
                for n, term in enumerate(terms):
                    total[tile][n] = term if total[tile][n] is None else total[tile][n] + term

            for j in range(4):
                near = [pick(position, [t[part][(p - j) % 4] for p in range(4)]) for part in (0, 1)]
                far = [pick(position, [t[part][(p - j) % 4] for p in range(4)]) for part in (2, 3)]
                here = position >= j
                shifted = [jnp.where(here, s[part][j], 0.0) for part in (0, 1)]
                mixed = [jnp.where(here, s[part + 2][j], s[part][j]) for part in (0, 1)]
                add(0, near, shifted)
                add(1, near, mixed)
                add(1, far, shifted)
            prods = []
            for rr, ii, ri, ir in total:
                if step == 0:
                    special = jnp.logical_and(first_row, i == 0)
                    pair = (rr - jnp.where(special, 0.0, ii), jnp.where(special, ii, ri + ir))
                else:
                    pair = (rr - ii, ri + ir)
                prods.append(pair)
            for part, dst in enumerate((re, im)):
                p0, p1 = prods[0][part], prods[1][part]
                q0, q1 = pltpu.roll(p0, 32, 1), pltpu.roll(p1, 32, 1)
                prod[dst, left] = p0 + sign * jnp.where(position >= 1, q0, 0.0)
                prod[dst, right] = p1 + sign * jnp.where(position >= 1, q1, q0)
            return carry

        lax.fori_loop(0, FREQS // rows, body, 0, unroll=8)
        whole = prod[...]
        high = whole.astype(bf16)
        low = (whole - high.astype(f32)).astype(bf16)
        copies[2 * step + 1].wait()
        part = dot(back[step, 0], high) + dot(back[step, 1], high) + dot(back[step, 0], low)
        acc[...] = part if step == 0 else acc[...] + part

    my_h, my_y = lax.axis_index("h"), lax.axis_index("y")
    for h in range(2):
        for kk in range(2):
            blocks = [
                acc[kk * 256 + r * 64 : kk * 256 + (r + 1) * 64, h * 128 : (h + 1) * 128]
                for r in range(4)
            ]
            for y, block in enumerate(swap_groups(blocks)):
                spread[h, y, kk] = block.astype(bf16)
    for shift, out_ref in enumerate(out_refs):
        for far in range(2):
            out_ref[far] = spread[(my_h + far) % 2, (my_y + shift) % 4]


def gate_kernel(far, *refs):
    parts, (q0, k0, v0, q1, k1, v1, bias_ref, out_ref, held) = refs[:4], refs[4:]
    my_h, my_y, my_k = lax.axis_index("h"), lax.axis_index("y"), lax.axis_index("k")
    for shift, part in enumerate(parts):
        held[(my_y - shift + 4) % 4] = part[...]
    col = pl.multiple_of((my_k * 2 + (my_h + far) % 2) * 128, 128)
    cols = pl.ds(col, 128)
    bias = bias_ref[:, cols]
    for own, (q, k, v) in enumerate(((q0, k0, v0), (q1, k1, v1))):
        kk = (my_k + own) % 2
        blocks = swap_groups([held[y, kk].astype(f32) for y in range(4)])
        for r, conv in enumerate(blocks):
            rows = slice(r * 64, (r + 1) * 64)
            signal = k[rows, cols].astype(f32) * v[rows, cols].astype(f32)
            out_ref[own, rows, :] = (q[rows, cols].astype(f32) * (conv + bias * signal)).astype(bf16)


def project_kernel(far, last, *refs):
    g, w, rest = refs[:5], refs[5:15], refs[15:]
    if last:
        before, own_ref, other_ref, lhs, rhs, sems = rest
    else:
        out_ref, lhs, rhs, sems = rest
    ax = {a: lax.axis_index(a) for a in AXES}
    half = pl.multiple_of(((ax["h"] + far) % 2) * 128, 128)
    swapped = (ax["k"] + ax["l"]) % 2
    places = ((0, (0, 1)), (3, (0, 1)), (1, (0, 1)), (2, (0,)), (2, (1,)))
    pairs = []
    for dh in range(2):
        for which, (dy, parts) in enumerate(places):
            src = w[dh * 5 + which]
            h, y = (ax["h"] + dh) % 2, (ax["y"] + dy) % 4
            row = pl.multiple_of((h * 4 + y) * 128, 128)
            for p in parts:
                col = pl.multiple_of(((swapped + p) % 2) * 512, 512)
                piece = src.at[p] if len(parts) == 2 else src
                pairs.append((piece.at[pl.ds(half, 128)], rhs.at[pl.ds(row, 128), pl.ds(col, 512)]))
    for which, (dx, parts) in enumerate(places):
        x = (ax["x"] + dx) % 4
        for p in parts:
            piece = g[which].at[p] if len(parts) == 2 else g[which]
            for j in range(2):
                pair = (ax["l"] // 2 + j) % 2
                col = pl.multiple_of((x * 2 + pair) * 128, 128)
                pairs.append((piece.at[j], lhs.at[pl.ds(p * 256, 256), pl.ds(col, 128)]))
    for copy in fetch(pairs, sems):
        copy.wait()

    def tile(i, carry):
        rows = pl.ds(pl.multiple_of(i * 128, 128), 128)
        part = jnp.dot(lhs[rows, :], rhs[...], preferred_element_type=f32)
        if last:
            here = pl.ds(pl.multiple_of((i % 2) * 128, 128), 128)

            @pl.when(i < 2)
            def _():
                own_ref[here, :] = before[rows, :] + part

            @pl.when(i >= 2)
            def _():
                other_ref[here, :] = before[rows, :] + part
        else:
            out_ref[rows, :] = part
        return carry

    lax.fori_loop(0, 4, tile, 0)


VMEM = pl.BlockSpec(memory_space=pltpu.VMEM)
ANY = pl.BlockSpec(memory_space=pl.ANY)


def params(limit=48 * MIB, **kw):
    return pltpu.CompilerParams(vmem_limit_bytes=limit, **kw)


def pack(key_in, value_in, taps):
    return pl.pallas_call(
        pack_kernel,
        out_shape=jax.ShapeDtypeStruct((2, 4, 2, 2, 64, 128), bf16),
        in_specs=[ANY] * 3,
        out_specs=VMEM,
        scratch_shapes=[
            pltpu.VMEM((256, 512), bf16),
            pltpu.VMEM((256, 512), bf16),
            pltpu.VMEM((256, 512), f32),
            pltpu.SemaphoreType.DMA((3,)),
        ],
        compiler_params=params(),
        name="pack",
    )(key_in, value_in, taps)


def convolve(received):
    fwd, back = transform_tables()
    return pl.pallas_call(
        conv_kernel,
        out_shape=[jax.ShapeDtypeStruct((2, 2, 64, 128), bf16)] * 4,
        in_specs=[VMEM, ANY, ANY],
        out_specs=[VMEM] * 4,
        scratch_shapes=[
            pltpu.VMEM(fwd.shape, bf16),
            pltpu.VMEM(back.shape, bf16),
            pltpu.VMEM((512, 512), bf16),
            pltpu.VMEM((2 * FREQS, 512), f32),
            pltpu.VMEM((2 * FREQS, 256), f32),
            pltpu.VMEM((512, 256), f32),
            pltpu.VMEM((2, 4, 2, 64, 128), bf16),
            pltpu.SemaphoreType.DMA((2 * STEPS,)),
        ],
        compiler_params=params(),
        name="convolve",
    )(received, jnp.asarray(fwd), jnp.asarray(back))


def gate(far, parts, own, partner, bias):
    return pl.pallas_call(
        functools.partial(gate_kernel, far),
        out_shape=jax.ShapeDtypeStruct((2, 256, 128), bf16),
        in_specs=[VMEM] * 11,
        out_specs=VMEM,
        scratch_shapes=[pltpu.VMEM((4, 2, 64, 128), bf16)],
        compiler_params=params(),
        name="gate",
    )(*parts, *own, *partner, bias)


def project(far, gated, weights, before=None):
    last = before is not None
    half = jax.ShapeDtypeStruct((256, 1024), f32)
    return pl.pallas_call(
        functools.partial(project_kernel, far, last),
        out_shape=[half] * 2 if last else jax.ShapeDtypeStruct((512, 1024), f32),
        in_specs=[ANY] * 15 + [VMEM] * last,
        out_specs=[VMEM] * 2 if last else VMEM,
        scratch_shapes=[
            pltpu.VMEM((512, 1024), bf16),
            pltpu.VMEM((1024, 1024), bf16),
            pltpu.SemaphoreType.DMA((32,)),
        ],
        compiler_params=params(),
        name="project",
    )(*gated, *weights, *([before] if last else []))


def shift(v, axis, by):
    n = lax.axis_size(axis)
    return lax.ppermute(v, axis, [(i, (i + by) % n) for i in range(n)])


def ring(v, axis):
    up, down = shift(v, axis, 1), shift(v, axis, -1)
    return [v, up, down, shift(up[0], axis, 1), shift(down[1], axis, -1)]


def gather_gated(v):
    partner = lax.ppermute(v, "l", [(i, i ^ 2) for i in range(4)])
    return ring(jnp.stack([v, partner], axis=1), "x")


def body(query, key_in, value_in, filter_taps, conv_bias, out_weight):
    core = lax.axis_index("k")
    own = (query, key_in, value_in)
    packed = pack(key_in, value_in, filter_taps).reshape(16, 2, 64, 128)
    partner = tuple(shift(v, "k", 1) for v in own)

    swaps = []
    for k in range(2):
        for l in range(4):
            to = (k, l) if k == l % 2 else (1 - k, l ^ 1)
            swaps.append((k * 4 + l, to[0] * 4 + to[1]))
    out_weight = lax.ppermute(out_weight, ("k", "l"), swaps)
    keep = lax.dynamic_slice(out_weight, (core * 256, 0), (256, 512))
    give = lax.dynamic_slice(out_weight, ((1 - core) * 256, 0), (256, 512))
    weight = jnp.stack([keep, shift(give, "k", 1)])

    received = lax.all_to_all(packed, SEQ, split_axis=0, concat_axis=0, tiled=True)
    weights = ring(weight, "y")
    received, partner, weights = lax.optimization_barrier((received, partner, weights))
    across = shift(weights[0], "h", 1)

    to_y = convolve(received)
    parts = [to_y[0]] + [shift(to_y[s], "y", s) for s in (1, 2, 3)]
    parts = lax.optimization_barrier(parts)
    crossing = shift(jnp.stack([p[1] for p in parts]), "h", 1)
    bias = conv_bias.reshape(1, 512)
    near = gather_gated(gate(0, [p[0] for p in parts], own, partner, bias))
    weights = weights + ring(across, "y")
    far = gather_gated(gate(1, [crossing[s] for s in range(4)], own, partner, bias))

    half = project(0, near, weights)
    mine, other = project(1, far, weights, half)
    total = mine + shift(other, "k", 1)
    beside = lax.ppermute(total[:, 512:].astype(bf16), "l", [(i, i ^ 1) for i in range(4)])
    return (total[:, :512] + beside.astype(f32)).astype(bf16)


def solution(mesh):
    fine = Mesh(mesh.devices.reshape(2, 4, 2, 4, 4), AXES)
    block = P(SEQ, CHAN)
    return jax.shard_map(
        body,
        mesh=fine,
        in_specs=(block, block, block, block, P(CHAN), block),
        out_specs=block,
        check_vma=False,
    )
```

```python
import functools

import jax
import jax.numpy as jnp
import numpy as np
from jax import lax
from jax.experimental import pallas as pl
from jax.experimental.pallas import tpu as pltpu
from jax.sharding import Mesh
from jax.sharding import PartitionSpec as P

bf16 = jnp.bfloat16
f32 = jnp.float32
AXES = ("h", "y", "k", "x", "l")
SEQ = ("h", "y", "k")
CHAN = ("x", "l")
N = 1024
STEPS = 4
FREQS = 128
MIB = 1 << 20
LARGE = 60 * MIB


def transform_tables():
    k = np.arange(N // 2)[:, None]
    a = np.arange(N // 2)[None, :]
    angle = 2.0 * np.pi * ((k * a) % N) / N
    re, im = np.cos(angle), -np.sin(angle)
    im[0] = 1.0 - 2.0 * (np.arange(N // 2) % 2)
    weight = np.full((N // 2, 1), 2.0 / N)
    weight[0] = 1.0 / N
    forward = np.concatenate([re.reshape(STEPS, FREQS, -1), im.reshape(STEPS, FREQS, -1)], 1)
    back = np.concatenate(
        [(re * weight).reshape(STEPS, FREQS, -1), (im * weight).reshape(STEPS, FREQS, -1)], 1
    ).transpose(0, 2, 1)

    def split(m):
        high = m.astype(np.float32).astype(jnp.bfloat16)
        low = (m - high.astype(np.float64)).astype(np.float32).astype(jnp.bfloat16)
        return np.stack([high, low], 1)

    return split(forward), split(back)


def lanes(rows):
    return lax.broadcasted_iota(jnp.int32, (rows, 128), 1)


def swap_groups(blocks):
    a0, a1, a2, a3 = blocks
    lane = lanes(a0.shape[0])
    low, even = lane < 64, (lane & 32) == 0
    roll = lambda v, n: pltpu.roll(v, n, 1)
    b0, b2 = jnp.where(low, a0, roll(a2, 64)), jnp.where(low, roll(a0, 64), a2)
    b1, b3 = jnp.where(low, a1, roll(a3, 64)), jnp.where(low, roll(a1, 64), a3)
    c0, c1 = jnp.where(even, b0, roll(b1, 32)), jnp.where(even, roll(b0, 96), b1)
    c2, c3 = jnp.where(even, b2, roll(b3, 32)), jnp.where(even, roll(b2, 96), b3)
    return c0, c1, c2, c3


def fetch(pairs, sems):
    copies = [pltpu.make_async_copy(src, dst, sems.at[i]) for i, (src, dst) in enumerate(pairs)]
    for copy in copies:
        copy.start()
    return copies


def pack_kernel(query_hbm, key_hbm, value_hbm, taps_hbm, out_ref, keep_ref, give_ref, *scratch):
    query_ref, key_ref, value_ref, taps_ref, sems = scratch
    pairs = (
        (taps_hbm, taps_ref),
        (key_hbm, key_ref),
        (value_hbm, value_ref),
        (query_hbm, query_ref),
    )
    copies = fetch(pairs, sems)
    core = lax.axis_index("k")

    def scatter(which, read):
        for v in range(4):
            cols = slice(v * 128, (v + 1) * 128)
            blocks = swap_groups([read(slice(r * 64, (r + 1) * 64), cols) for r in range(4)])
            for y, block in enumerate(blocks):
                out_ref[v % 2, y, v // 2, which] = block.astype(bf16)

    copies[0].wait()
    scatter(1, lambda rows, cols: taps_ref[rows, cols])
    copies[1].wait()
    copies[2].wait()
    scatter(0, lambda rows, cols: key_ref[rows, cols].astype(f32) * value_ref[rows, cols].astype(f32))
    copies[3].wait()
    for i, ref in enumerate((query_ref, key_ref, value_ref)):
        for dst, half in ((keep_ref, core), (give_ref, 1 - core)):
            dst[i] = ref[:, pl.ds(pl.multiple_of(half * 256, 256), 256)]


def pick(position, choices):
    return jnp.where(
        position == 0,
        choices[0],
        jnp.where(position == 1, choices[1], jnp.where(position == 2, choices[2], choices[3])),
    )


def conv_kernel(in_ref, fwd_hbm, back_hbm, *refs):
    out_ref, fwd, back, both, spec, prod, acc, sems = refs
    tables = []
    for i in range(STEPS):
        tables += [(fwd_hbm.at[i], fwd.at[i]), (back_hbm.at[i], back.at[i])]
    copies = fetch(tables, sems)
    for which in range(2):
        for h in range(2):
            for kk in range(2):
                blocks = [in_ref[h * 8 + y * 2 + kk, which].astype(f32) for y in range(4)]
                for r, block in enumerate(swap_groups(blocks)):
                    row, col = kk * 256 + r * 64, which * 256 + h * 128
                    both[row : row + 64, col : col + 128] = block.astype(bf16)

    dot = functools.partial(jnp.dot, preferred_element_type=f32)
    rows = 8
    position = lanes(rows) // 32
    row_id = lax.broadcasted_iota(jnp.int32, (rows, 128), 0)
    sign = (1 - 2 * (row_id & 1)).astype(f32)
    first_row = row_id == 0

    def rolled(v):
        return [v] + [pltpu.roll(v, 32 * i, 1) for i in (1, 2, 3)]

    for step in range(STEPS):
        copies[2 * step].wait()
        spec[...] = dot(fwd[step, 0], both[...]) + dot(fwd[step, 1], both[...])

        def body(i, carry, step=step):
            base = pl.multiple_of(i * rows, rows)
            re, im = pl.ds(base, rows), pl.ds(base + FREQS, rows)
            left, right = slice(0, 128), slice(128, 256)
            s = [rolled(spec[part, side]) for side in (left, right) for part in (re, im)]
            left_t, right_t = slice(256, 384), slice(384, 512)
            t = [rolled(spec[part, side]) for side in (left_t, right_t) for part in (re, im)]
            total = [[None] * 4 for _ in range(2)]

            def add(tile, tap, src):
                terms = (tap[0] * src[0], tap[1] * src[1], tap[1] * src[0], tap[0] * src[1])
                for n, term in enumerate(terms):
                    total[tile][n] = term if total[tile][n] is None else total[tile][n] + term

            for j in range(4):
                near = [pick(position, [t[part][(p - j) % 4] for p in range(4)]) for part in (0, 1)]
                far = [pick(position, [t[part][(p - j) % 4] for p in range(4)]) for part in (2, 3)]
                here = position >= j
                shifted = [jnp.where(here, s[part][j], 0.0) for part in (0, 1)]
                mixed = [jnp.where(here, s[part + 2][j], s[part][j]) for part in (0, 1)]
                add(0, near, shifted)
                add(1, near, mixed)
                add(1, far, shifted)
            prods = []
            for rr, ii, ri, ir in total:
                if step == 0:
                    special = jnp.logical_and(first_row, i == 0)
                    pair = (rr - jnp.where(special, 0.0, ii), jnp.where(special, ii, ri + ir))
                else:
                    pair = (rr - ii, ri + ir)
                prods.append(pair)
            for part, dst in enumerate((re, im)):
                p0, p1 = prods[0][part], prods[1][part]
                q0, q1 = pltpu.roll(p0, 32, 1), pltpu.roll(p1, 32, 1)
                prod[dst, left] = p0 + sign * jnp.where(position >= 1, q0, 0.0)
                prod[dst, right] = p1 + sign * jnp.where(position >= 1, q1, q0)
            return carry

        lax.fori_loop(0, FREQS // rows, body, 0, unroll=16)
        whole = prod[...]
        high = whole.astype(bf16)
        low = (whole - high.astype(f32)).astype(bf16)
        copies[2 * step + 1].wait()
        part = dot(back[step, 0], high) + dot(back[step, 1], high) + dot(back[step, 0], low)
        acc[...] = part if step == 0 else acc[...] + part

    for h in range(2):
        for kk in range(2):
            blocks = [
                acc[kk * 256 + r * 64 : kk * 256 + (r + 1) * 64, h * 128 : (h + 1) * 128]
                for r in range(4)
            ]
            for y, block in enumerate(swap_groups(blocks)):
                out_ref[h * 4 + y, kk] = block.astype(bf16)


def gate_kernel(in_ref, own_ref, partner_ref, bias_ref, out_ref):
    core = lax.axis_index("k")
    for h in range(2):
        cols = slice(h * 128, (h + 1) * 128)
        bias = bias_ref[:, pl.ds(pl.multiple_of(core * 256 + h * 128, 128), 128)]
        for other, ref in enumerate((own_ref, partner_ref)):
            kk = (core + other) % 2
            blocks = swap_groups([in_ref[h * 4 + y, kk].astype(f32) for y in range(4)])
            for r, conv in enumerate(blocks):
                rows = slice(r * 64, (r + 1) * 64)
                q, k, v = [ref[i, rows, cols].astype(f32) for i in range(3)]
                out_ref[other, rows, cols] = (q * (conv + bias * (k * v))).astype(bf16)


PIECES = [(0, dy, p) for dy in (0, 3, 1, 2) for p in (0, 1)]
PIECES += [(1, dy, p) for dy in (0, 3, 1) for p in (0, 1)] + [(1, 2, 0), (1, 2, 1)]


def beside(blocks, p):
    return jnp.concatenate([block[p] for block in blocks], axis=1)


def first_kernel(*refs):
    gated, weights, outs = refs[:4], refs[4:13], refs[13:]
    mine_ref, other_ref, rest_mine, rest_other, rhs, sems = outs
    at = {a: lax.axis_index(a) for a in AXES}
    swapped = (at["k"] + at["l"]) % 2
    pairs = []
    for i, (dh, dy, p) in enumerate(PIECES):
        h, y = (at["h"] + dh) % 2, (at["y"] + dy) % 4
        rest = (y + at["l"] // 2) % 2
        x = (2 * h + y // 2 - at["x"] + 4) % 4
        rows = pl.ds(pl.multiple_of(rest * 1024 + x * 256, 256), 256)
        cols = pl.ds(pl.multiple_of(((swapped + p) % 2) * 512, 512), 512)
        piece = weights[7 + p] if i >= 14 else weights[i // 2].at[p]
        pairs.append((piece, rhs.at[rows, cols]))
    for copy in fetch(pairs, sems):
        copy.wait()
    for p in range(2):
        lhs = beside(gated, p)
        for col, ref in enumerate((mine_ref, other_ref)):
            cols = slice(col * 512, (col + 1) * 512)
            ref[p] = jnp.dot(lhs, rhs[:1024, cols], preferred_element_type=f32)
    rest_mine[...] = rhs[1024:, :512]
    rest_other[...] = rhs[1024:, 512:]


def rest_kernel(g0, g1, g2, g3, before, rhs, own_ref, other_ref):
    for p, ref in enumerate((own_ref, other_ref)):
        lhs = beside((g0, g1, g2, g3), p)
        ref[...] = before[p] + jnp.dot(lhs, rhs[...], preferred_element_type=f32)


VMEM = pl.BlockSpec(memory_space=pltpu.VMEM)
ANY = pl.BlockSpec(memory_space=pl.ANY)


def params(limit=48 * MIB, **kw):
    return pltpu.CompilerParams(vmem_limit_bytes=limit, **kw)


def cost(microseconds):
    rate = 1 << 30
    return pl.CostEstimate(flops=int(microseconds * rate), bytes_accessed=0, transcendentals=0)


def pack(query, key_in, value_in, taps):
    half = jax.ShapeDtypeStruct((3, 256, 256), bf16)
    return pl.pallas_call(
        pack_kernel,
        out_shape=[jax.ShapeDtypeStruct((2, 4, 2, 2, 64, 128), bf16), half, half],
        in_specs=[ANY] * 4,
        out_specs=[VMEM] * 3,
        scratch_shapes=[
            pltpu.VMEM((256, 512), bf16),
            pltpu.VMEM((256, 512), bf16),
            pltpu.VMEM((256, 512), bf16),
            pltpu.VMEM((256, 512), f32),
            pltpu.SemaphoreType.DMA((4,)),
        ],
        compiler_params=params(LARGE),
        cost_estimate=cost(2),
        name="pack",
    )(query, key_in, value_in, taps)


def convolve(received):
    fwd, back = transform_tables()
    return pl.pallas_call(
        conv_kernel,
        out_shape=jax.ShapeDtypeStruct((8, 2, 64, 128), bf16),
        in_specs=[VMEM, ANY, ANY],
        out_specs=VMEM,
        scratch_shapes=[
            pltpu.VMEM(fwd.shape, bf16),
            pltpu.VMEM(back.shape, bf16),
            pltpu.VMEM((512, 512), bf16),
            pltpu.VMEM((2 * FREQS, 512), f32),
            pltpu.VMEM((2 * FREQS, 256), f32),
            pltpu.VMEM((512, 256), f32),
            pltpu.SemaphoreType.DMA((2 * STEPS,)),
        ],
        compiler_params=params(LARGE),
        cost_estimate=cost(10),
        name="convolve",
    )(received, jnp.asarray(fwd), jnp.asarray(back))


def gate(conv, own, partner, bias):
    return pl.pallas_call(
        gate_kernel,
        out_shape=jax.ShapeDtypeStruct((2, 256, 256), bf16),
        in_specs=[VMEM] * 4,
        out_specs=VMEM,
        compiler_params=params(),
        cost_estimate=cost(1),
        name="gate",
    )(conv, own, partner, bias)


def project_first(gated, weights):
    part = jax.ShapeDtypeStruct((2, 256, 512), f32)
    rest = jax.ShapeDtypeStruct((1024, 512), bf16)
    return pl.pallas_call(
        first_kernel,
        out_shape=[part, part, rest, rest],
        in_specs=[VMEM] * 4 + [ANY] * 9,
        out_specs=[VMEM] * 4,
        scratch_shapes=[pltpu.VMEM((2048, 1024), bf16), pltpu.SemaphoreType.DMA((16,))],
        compiler_params=params(32 * MIB),
        cost_estimate=cost(5),
        name="project_first",
    )(*gated, *weights)


def project_rest(gated, before, rhs):
    half = jax.ShapeDtypeStruct((256, 512), f32)
    return pl.pallas_call(
        rest_kernel,
        out_shape=[half] * 2,
        in_specs=[VMEM] * 6,
        out_specs=[VMEM] * 2,
        compiler_params=params(32 * MIB),
        cost_estimate=cost(3),
        name="project_rest",
    )(*gated, before, rhs)


def shift(v, axis, by):
    n = lax.axis_size(axis)
    return lax.ppermute(v, axis, [(i, (i + by) % n) for i in range(n)])


def around(v, axis):
    return v, shift(v, axis, -1), shift(v, axis, 2), shift(v, axis, 1)


def body(query, key_in, value_in, filter_taps, conv_bias, out_weight):
    core = lax.axis_index("k")
    tie = lax.optimization_barrier
    bias = conv_bias.reshape(1, 512)
    packed, own, give = pack(query, key_in, value_in, filter_taps)
    received = lax.all_to_all(
        packed.reshape(16, 2, 64, 128), SEQ, split_axis=0, concat_axis=0, tiled=True
    )
    partner = shift(give, "k", 1)

    swaps = []
    for k in range(2):
        for l in range(4):
            to = (k, l) if k == l % 2 else (1 - k, l ^ 1)
            swaps.append((k * 4 + l, to[0] * 4 + to[1]))
    out_weight = lax.ppermute(out_weight, ("k", "l"), swaps)
    keep = lax.dynamic_slice(out_weight, (core * 256, 0), (256, 512))
    give = lax.dynamic_slice(out_weight, ((1 - core) * 256, 0), (256, 512))
    weight = jnp.stack([keep, shift(give, "k", 1)])
    down, two, up = around(weight, "y")[1:]
    across = shift(weight, "h", 1)
    received, partner, weight = tie((received, partner, weight))

    conv, up, down, two, across = tie((convolve(received), up, down, two, across))
    weights = (weight, up, down, two, across)
    conv = lax.all_to_all(conv, ("h", "y"), split_axis=0, concat_axis=0, tiled=True)
    up, down = shift(across, "y", 1), shift(across, "y", -1)
    mine = gate(conv, own, partner, bias)
    other = lax.ppermute(mine, "l", [(i, i ^ 2) for i in range(4)])
    mine, other, up, down = tie((around(mine, "x"), other, up, down))

    other = around(other, "x")
    weights += (up, down, shift(up[0], "y", 1), shift(down[1], "y", -1))
    half_mine, half_other, rest_mine, rest_other = project_first(mine, weights)
    other, half_mine, rest_mine = tie((other, half_mine, rest_mine))
    own, partner = project_rest(other, half_other, rest_other)
    send = (own + shift(partner, "k", 1)).astype(bf16)
    send, other, half_mine = tie((send, other, half_mine))
    from_pair = lax.ppermute(send, "l", [(i, i ^ 1) for i in range(4)])
    own, partner = project_rest(other, half_mine, rest_mine)
    return (own + shift(partner, "k", 1) + from_pair.astype(f32)).astype(bf16)


def solution(mesh):
    fine = Mesh(mesh.devices.reshape(2, 4, 2, 4, 4), AXES)
    block = P(SEQ, CHAN)
    return jax.shard_map(
        body,
        mesh=fine,
        in_specs=(block, block, block, block, P(CHAN), block),
        out_specs=block,
        check_vma=False,
    )
```

```python
import functools

import jax
import jax.numpy as jnp
import numpy as np
from jax import lax
from jax.experimental import pallas as pl
from jax.experimental.pallas import tpu as pltpu
from jax.sharding import Mesh
from jax.sharding import PartitionSpec as P

bf16 = jnp.bfloat16
f32 = jnp.float32
AXES = ("h", "y", "k", "x", "l")
SEQ = ("h", "y", "k")
CHAN = ("x", "l")
N = 1024
STEPS = 4
FREQS = 128
MIB = 1 << 20
LARGE = 60 * MIB


def transform_tables():
    k = np.arange(N // 2)[:, None]
    a = np.arange(N // 2)[None, :]
    angle = 2.0 * np.pi * ((k * a) % N) / N
    re, im = np.cos(angle), -np.sin(angle)
    im[0] = 1.0 - 2.0 * (np.arange(N // 2) % 2)
    weight = np.full((N // 2, 1), 2.0 / N)
    weight[0] = 1.0 / N
    forward = np.concatenate([re.reshape(STEPS, FREQS, -1), im.reshape(STEPS, FREQS, -1)], 1)
    back = np.concatenate(
        [(re * weight).reshape(STEPS, FREQS, -1), (im * weight).reshape(STEPS, FREQS, -1)], 1
    ).transpose(0, 2, 1)

    def split(m):
        high = m.astype(np.float32).astype(jnp.bfloat16)
        low = (m - high.astype(np.float64)).astype(np.float32).astype(jnp.bfloat16)
        return np.stack([high, low], 1)

    return split(forward), split(back)


def lanes(rows):
    return lax.broadcasted_iota(jnp.int32, (rows, 128), 1)


def swap_groups(blocks):
    a0, a1, a2, a3 = blocks
    lane = lanes(a0.shape[0])
    low, even = lane < 64, (lane & 32) == 0
    roll = lambda v, n: pltpu.roll(v, n, 1)
    b0, b2 = jnp.where(low, a0, roll(a2, 64)), jnp.where(low, roll(a0, 64), a2)
    b1, b3 = jnp.where(low, a1, roll(a3, 64)), jnp.where(low, roll(a1, 64), a3)
    c0, c1 = jnp.where(even, b0, roll(b1, 32)), jnp.where(even, roll(b0, 96), b1)
    c2, c3 = jnp.where(even, b2, roll(b3, 32)), jnp.where(even, roll(b2, 96), b3)
    return c0, c1, c2, c3


def fetch(pairs, sems):
    copies = [pltpu.make_async_copy(src, dst, sems.at[i]) for i, (src, dst) in enumerate(pairs)]
    for copy in copies:
        copy.start()
    return copies


def pack_kernel(key_hbm, value_hbm, taps_hbm, out_ref, key_ref, value_ref, taps_ref, sems):
    pairs = ((taps_hbm, taps_ref), (key_hbm, key_ref), (value_hbm, value_ref))
    copies = fetch(pairs, sems)

    def scatter(which, read):
        for v in range(4):
            cols = slice(v * 128, (v + 1) * 128)
            blocks = swap_groups([read(slice(r * 64, (r + 1) * 64), cols) for r in range(4)])
            for y, block in enumerate(blocks):
                out_ref[v % 2, y, v // 2, which] = block.astype(bf16)

    copies[0].wait()
    scatter(1, lambda rows, cols: taps_ref[rows, cols])
    copies[1].wait()
    copies[2].wait()
    scatter(0, lambda rows, cols: key_ref[rows, cols].astype(f32) * value_ref[rows, cols].astype(f32))


def pick(position, choices):
    return jnp.where(
        position == 0,
        choices[0],
        jnp.where(position == 1, choices[1], jnp.where(position == 2, choices[2], choices[3])),
    )


def conv_kernel(in_ref, bias_ref, fwd_hbm, back_hbm, *refs):
    out_ref, fwd, back, both, spec, prod, acc, sems = refs
    tables = []
    for i in range(STEPS):
        tables += [(fwd_hbm.at[i], fwd.at[i]), (back_hbm.at[i], back.at[i])]
    copies = fetch(tables, sems)
    for which in range(2):
        for h in range(2):
            for kk in range(2):
                blocks = [in_ref[h * 8 + y * 2 + kk, which].astype(f32) for y in range(4)]
                for r, block in enumerate(swap_groups(blocks)):
                    row, col = kk * 256 + r * 64, which * 256 + h * 128
                    both[row : row + 64, col : col + 128] = block.astype(bf16)

    dot = functools.partial(jnp.dot, preferred_element_type=f32)
    rows = 8
    position = lanes(rows) // 32
    row_id = lax.broadcasted_iota(jnp.int32, (rows, 128), 0)
    sign = (1 - 2 * (row_id & 1)).astype(f32)
    first_row = row_id == 0

    def rolled(v):
        return [v] + [pltpu.roll(v, 32 * i, 1) for i in (1, 2, 3)]

    start = lax.axis_index("k") * 256 + (lax.axis_index("h") * 4 + lax.axis_index("y")) * 32
    tile = pl.multiple_of(start // 128 * 128, 128)
    bias = pltpu.roll(bias_ref[:, pl.ds(tile, 128)], 128 - start % 128, 1)
    bias = jnp.where(lanes(1) < 32, bias, 0.0)

    for step in range(STEPS):
        copies[2 * step].wait()
        spec[...] = dot(fwd[step, 0], both[...]) + dot(fwd[step, 1], both[...])
        spec[:FREQS, 256:384] += bias
        if step == 0:
            spec[FREQS : FREQS + 1, 256:384] += bias

        def body(i, carry, step=step):
            base = pl.multiple_of(i * rows, rows)
            re, im = pl.ds(base, rows), pl.ds(base + FREQS, rows)
            left, right = slice(0, 128), slice(128, 256)
            s = [rolled(spec[part, side]) for side in (left, right) for part in (re, im)]
            left_t, right_t = slice(256, 384), slice(384, 512)
            t = [rolled(spec[part, side]) for side in (left_t, right_t) for part in (re, im)]
            total = [[None] * 4 for _ in range(2)]

            def add(tile, tap, src):
                terms = (tap[0] * src[0], tap[1] * src[1], tap[1] * src[0], tap[0] * src[1])
                for n, term in enumerate(terms):
                    total[tile][n] = term if total[tile][n] is None else total[tile][n] + term

            for j in range(4):
                near = [pick(position, [t[part][(p - j) % 4] for p in range(4)]) for part in (0, 1)]
                far = [pick(position, [t[part][(p - j) % 4] for p in range(4)]) for part in (2, 3)]
                here = position >= j
                shifted = [jnp.where(here, s[part][j], 0.0) for part in (0, 1)]
                mixed = [jnp.where(here, s[part + 2][j], s[part][j]) for part in (0, 1)]
                add(0, near, shifted)
                add(1, near, mixed)
                add(1, far, shifted)
            prods = []
            for rr, ii, ri, ir in total:
                if step == 0:
                    special = jnp.logical_and(first_row, i == 0)
                    pair = (rr - jnp.where(special, 0.0, ii), jnp.where(special, ii, ri + ir))
                else:
                    pair = (rr - ii, ri + ir)
                prods.append(pair)
            for part, dst in enumerate((re, im)):
                p0, p1 = prods[0][part], prods[1][part]
                q0, q1 = pltpu.roll(p0, 32, 1), pltpu.roll(p1, 32, 1)
                prod[dst, left] = p0 + sign * jnp.where(position >= 1, q0, 0.0)
                prod[dst, right] = p1 + sign * jnp.where(position >= 1, q1, q0)
            return carry

        lax.fori_loop(0, FREQS // rows, body, 0, unroll=16)
        whole = prod[...]
        high = whole.astype(bf16)
        low = (whole - high.astype(f32)).astype(bf16)
        copies[2 * step + 1].wait()
        part = dot(back[step, 0], high) + dot(back[step, 1], high) + dot(back[step, 0], low)
        acc[...] = part if step == 0 else acc[...] + part

    for h in range(2):
        for kk in range(2):
            blocks = [
                acc[kk * 256 + r * 64 : kk * 256 + (r + 1) * 64, h * 128 : (h + 1) * 128]
                for r in range(4)
            ]
            for y, block in enumerate(swap_groups(blocks)):
                out_ref[h * 4 + y, kk] = block.astype(bf16)


def gate_kernel(in_ref, own_ref, partner_ref, out_ref):
    core = lax.axis_index("k")
    for h in range(2):
        cols = slice(h * 128, (h + 1) * 128)
        own_cols = pl.ds(pl.multiple_of(core * 256 + h * 128, 128), 128)
        for other, (ref, at) in enumerate(((own_ref, own_cols), (partner_ref, cols))):
            kk = (core + other) % 2
            blocks = swap_groups([in_ref[h * 4 + y, kk].astype(f32) for y in range(4)])
            for r, conv in enumerate(blocks):
                rows = slice(r * 64, (r + 1) * 64)
                out_ref[other, rows, cols] = (ref[rows, at].astype(f32) * conv).astype(bf16)


PIECES = [(dh, dy, p) for dh in (0, 1) for dy in (0, 1, 2, 3) for p in (0, 1)]


def beside(blocks, p):
    return jnp.concatenate([block[p] for block in blocks], axis=1)


def first_kernel(*refs):
    gated, weights, outs = refs[:4], refs[4:12], refs[12:]
    mine_ref, other_ref, rest_mine, rest_other, rhs, sems = outs
    at = {a: lax.axis_index(a) for a in AXES}
    swapped = (at["k"] + at["l"]) % 2
    pairs = []
    for i, (dh, dy, p) in enumerate(PIECES):
        h, y = (at["h"] + dh) % 2, (at["y"] + dy) % 4
        rest = (y + at["l"] // 2) % 2
        x = (2 * h + y // 2 - at["x"] + 4) % 4
        rows = pl.ds(pl.multiple_of(rest * 1024 + x * 256, 256), 256)
        cols = pl.ds(pl.multiple_of(((swapped + p) % 2) * 512, 512), 512)
        pairs.append((weights[i // 2].at[p], rhs.at[rows, cols]))
    for copy in fetch(pairs, sems):
        copy.wait()
    for p in range(2):
        lhs = beside(gated, p)
        for col, ref in enumerate((mine_ref, other_ref)):
            cols = slice(col * 512, (col + 1) * 512)
            ref[p] = jnp.dot(lhs, rhs[:1024, cols], preferred_element_type=f32)
    rest_mine[...] = rhs[1024:, :512]
    rest_other[...] = rhs[1024:, 512:]


def rest_kernel(g0, g1, g2, g3, before, rhs, own_ref, other_ref):
    for p, ref in enumerate((own_ref, other_ref)):
        lhs = beside((g0, g1, g2, g3), p)
        ref[...] = before[p] + jnp.dot(lhs, rhs[...], preferred_element_type=f32)


VMEM = pl.BlockSpec(memory_space=pltpu.VMEM)
ANY = pl.BlockSpec(memory_space=pl.ANY)


def params(limit=48 * MIB, **kw):
    return pltpu.CompilerParams(vmem_limit_bytes=limit, **kw)


def cost(microseconds):
    rate = 1 << 30
    return pl.CostEstimate(flops=int(microseconds * rate), bytes_accessed=0, transcendentals=0)


def pack(key_in, value_in, taps):
    return pl.pallas_call(
        pack_kernel,
        out_shape=jax.ShapeDtypeStruct((2, 4, 2, 2, 64, 128), bf16),
        in_specs=[ANY] * 3,
        out_specs=VMEM,
        scratch_shapes=[
            pltpu.VMEM((256, 512), bf16),
            pltpu.VMEM((256, 512), bf16),
            pltpu.VMEM((256, 512), f32),
            pltpu.SemaphoreType.DMA((3,)),
        ],
        compiler_params=params(LARGE),
        cost_estimate=cost(2),
        name="pack",
    )(key_in, value_in, taps)


def convolve(received, bias):
    fwd, back = transform_tables()
    return pl.pallas_call(
        conv_kernel,
        out_shape=jax.ShapeDtypeStruct((8, 2, 64, 128), bf16),
        in_specs=[VMEM, VMEM, ANY, ANY],
        out_specs=VMEM,
        scratch_shapes=[
            pltpu.VMEM(fwd.shape, bf16),
            pltpu.VMEM(back.shape, bf16),
            pltpu.VMEM((512, 512), bf16),
            pltpu.VMEM((2 * FREQS, 512), f32),
            pltpu.VMEM((2 * FREQS, 256), f32),
            pltpu.VMEM((512, 256), f32),
            pltpu.SemaphoreType.DMA((2 * STEPS,)),
        ],
        compiler_params=params(LARGE),
        cost_estimate=cost(10),
        name="convolve",
    )(received, bias, jnp.asarray(fwd), jnp.asarray(back))


def gate(conv, own, partner):
    return pl.pallas_call(
        gate_kernel,
        out_shape=jax.ShapeDtypeStruct((2, 256, 256), bf16),
        in_specs=[VMEM] * 3,
        out_specs=VMEM,
        compiler_params=params(),
        cost_estimate=cost(1),
        name="gate",
    )(conv, own, partner)


def project_first(gated, weights):
    part = jax.ShapeDtypeStruct((2, 256, 512), f32)
    rest = jax.ShapeDtypeStruct((1024, 512), bf16)
    return pl.pallas_call(
        first_kernel,
        out_shape=[part, part, rest, rest],
        in_specs=[VMEM] * 4 + [ANY] * 8,
        out_specs=[VMEM] * 4,
        scratch_shapes=[pltpu.VMEM((2048, 1024), bf16), pltpu.SemaphoreType.DMA((16,))],
        compiler_params=params(32 * MIB),
        cost_estimate=cost(5),
        name="project_first",
    )(*gated, *weights)


def project_rest(gated, before, rhs):
    half = jax.ShapeDtypeStruct((256, 512), f32)
    return pl.pallas_call(
        rest_kernel,
        out_shape=[half] * 2,
        in_specs=[VMEM] * 6,
        out_specs=[VMEM] * 2,
        compiler_params=params(32 * MIB),
        cost_estimate=cost(3),
        name="project_rest",
    )(*gated, before, rhs)


def shift(v, axis, by):
    n = lax.axis_size(axis)
    return lax.ppermute(v, axis, [(i, (i + by) % n) for i in range(n)])


def around(v, axis):
    return v, shift(v, axis, -1), shift(v, axis, 2), shift(v, axis, 1)


def body(query, key_in, value_in, filter_taps, conv_bias, out_weight):
    core = lax.axis_index("k")
    tie = lax.optimization_barrier
    bias = conv_bias.reshape(1, 512)
    packed = pack(key_in, value_in, filter_taps)
    received = lax.all_to_all(
        packed.reshape(16, 2, 64, 128), SEQ, split_axis=0, concat_axis=0, tiled=True
    )
    other_half = lax.dynamic_slice(query, (0, (1 - core) * 256), (256, 256))
    partner = shift(other_half, "k", 1)

    swaps = []
    for k in range(2):
        for l in range(4):
            to = (k, l) if k == l % 2 else (1 - k, l ^ 1)
            swaps.append((k * 4 + l, to[0] * 4 + to[1]))
    out_weight = lax.ppermute(out_weight, ("k", "l"), swaps)
    keep = lax.dynamic_slice(out_weight, (core * 256, 0), (256, 512))
    give = lax.dynamic_slice(out_weight, ((1 - core) * 256, 0), (256, 512))
    weight = jnp.stack([keep, shift(give, "k", 1)])
    up, down = shift(weight, "y", 1), shift(weight, "y", -1)
    received, partner, weight = tie((received, partner, weight))

    across = shift(weight, "h", 1)
    conv, up, down, weight = tie((convolve(received, bias), up, down, weight))
    two = shift(weight, "y", 2)
    conv = lax.all_to_all(conv, ("h", "y"), split_axis=0, concat_axis=0, tiled=True)
    two_over = shift(across, "y", 2)
    conv, across, two = tie((conv, across, two))
    weights = (weight, down, two, up)

    mine = gate(conv, query, partner)
    other = lax.ppermute(mine, "l", [(i, i ^ 2) for i in range(4)])
    mine, other, across, two = tie((around(mine, "x"), other, across, two_over))
    other = around(other, "x")
    weights += (across, shift(across, "y", -1), two, shift(across, "y", 1))
    half_mine, half_other, rest_mine, rest_other = project_first(mine, weights)
    other, half_mine, rest_mine = tie((other, half_mine, rest_mine))
    own, partner = project_rest(other, half_other, rest_other)
    send = (own + shift(partner, "k", 1)).astype(bf16)
    from_pair = lax.ppermute(send, "l", [(i, i ^ 1) for i in range(4)])
    own, partner = project_rest(other, half_mine, rest_mine)
    total, from_pair = tie((own + shift(partner, "k", 1), from_pair))
    return (total + from_pair.astype(f32)).astype(bf16)


def solution(mesh):
    fine = Mesh(mesh.devices.reshape(2, 4, 2, 4, 4), AXES)
    block = P(SEQ, CHAN)
    return jax.shard_map(
        body,
        mesh=fine,
        in_specs=(block, block, block, block, P(CHAN), block),
        out_specs=block,
        check_vma=False,
    )
```

```python
import functools

import jax
import jax.numpy as jnp
import numpy as np
from jax import lax
from jax.experimental import pallas as pl
from jax.experimental.pallas import tpu as pltpu
from jax.sharding import Mesh
from jax.sharding import PartitionSpec as P

bf16 = jnp.bfloat16
f32 = jnp.float32
AXES = ("h", "y", "k", "x", "l")
SEQ = ("h", "y", "k")
CHAN = ("x", "l")
N = 1024
STEPS = 4
FREQS = 128
MIB = 1 << 20
LARGE = 60 * MIB


def transform_tables():
    k = np.arange(N // 2)[:, None]
    a = np.arange(N // 2)[None, :]
    angle = 2.0 * np.pi * ((k * a) % N) / N
    re, im = np.cos(angle), -np.sin(angle)
    im[0] = 1.0 - 2.0 * (np.arange(N // 2) % 2)
    weight = np.full((N // 2, 1), 2.0 / N)
    weight[0] = 1.0 / N
    forward = np.concatenate([re.reshape(STEPS, FREQS, -1), im.reshape(STEPS, FREQS, -1)], 1)
    back = np.concatenate(
        [(re * weight).reshape(STEPS, FREQS, -1), (im * weight).reshape(STEPS, FREQS, -1)], 1
    ).transpose(0, 2, 1)

    def split(m):
        high = m.astype(np.float32).astype(jnp.bfloat16)
        low = (m - high.astype(np.float64)).astype(np.float32).astype(jnp.bfloat16)
        return np.stack([high, low], 1)

    return split(forward), split(back)


def lanes(rows):
    return lax.broadcasted_iota(jnp.int32, (rows, 128), 1)


def swap_groups(blocks):
    a0, a1, a2, a3 = blocks
    lane = lanes(a0.shape[0])
    low, even = lane < 64, (lane & 32) == 0
    roll = lambda v, n: pltpu.roll(v, n, 1)
    b0, b2 = jnp.where(low, a0, roll(a2, 64)), jnp.where(low, roll(a0, 64), a2)
    b1, b3 = jnp.where(low, a1, roll(a3, 64)), jnp.where(low, roll(a1, 64), a3)
    c0, c1 = jnp.where(even, b0, roll(b1, 32)), jnp.where(even, roll(b0, 96), b1)
    c2, c3 = jnp.where(even, b2, roll(b3, 32)), jnp.where(even, roll(b2, 96), b3)
    return c0, c1, c2, c3


def fetch(pairs, sems):
    copies = [pltpu.make_async_copy(src, dst, sems.at[i]) for i, (src, dst) in enumerate(pairs)]
    for copy in copies:
        copy.start()
    return copies


def pack_kernel(key_hbm, value_hbm, taps_hbm, out_ref, key_ref, value_ref, taps_ref, sems):
    pairs = ((taps_hbm, taps_ref), (key_hbm, key_ref), (value_hbm, value_ref))
    copies = fetch(pairs, sems)

    def scatter(which, read):
        for v in range(4):
            cols = slice(v * 128, (v + 1) * 128)
            blocks = swap_groups([read(slice(r * 64, (r + 1) * 64), cols) for r in range(4)])
            for y, block in enumerate(blocks):
                out_ref[v % 2, y, v // 2, which] = block.astype(bf16)

    copies[0].wait()
    scatter(1, lambda rows, cols: taps_ref[rows, cols])
    copies[1].wait()
    copies[2].wait()
    scatter(0, lambda rows, cols: key_ref[rows, cols].astype(f32) * value_ref[rows, cols].astype(f32))


def pick(position, choices):
    return jnp.where(
        position == 0,
        choices[0],
        jnp.where(position == 1, choices[1], jnp.where(position == 2, choices[2], choices[3])),
    )


def conv_kernel(in_ref, bias_ref, fwd_hbm, back_hbm, *refs):
    out_ref, fwd, back, both, spec, prod, acc, sems = refs
    tables = []
    for i in range(STEPS):
        tables += [(fwd_hbm.at[i], fwd.at[i]), (back_hbm.at[i], back.at[i])]
    copies = fetch(tables, sems)
    for which in range(2):
        for h in range(2):
            for kk in range(2):
                blocks = [in_ref[h * 8 + y * 2 + kk, which].astype(f32) for y in range(4)]
                for r, block in enumerate(swap_groups(blocks)):
                    row, col = kk * 256 + r * 64, which * 256 + h * 128
                    both[row : row + 64, col : col + 128] = block.astype(bf16)

    dot = functools.partial(jnp.dot, preferred_element_type=f32)
    rows = 8
    position = lanes(rows) // 32
    row_id = lax.broadcasted_iota(jnp.int32, (rows, 128), 0)
    sign = (1 - 2 * (row_id & 1)).astype(f32)
    first_row = row_id == 0

    def rolled(v):
        return [v] + [pltpu.roll(v, 32 * i, 1) for i in (1, 2, 3)]

    start = lax.axis_index("k") * 256 + (lax.axis_index("h") * 4 + lax.axis_index("y")) * 32
    tile = pl.multiple_of(start // 128 * 128, 128)
    bias = pltpu.roll(bias_ref[:, pl.ds(tile, 128)], 128 - start % 128, 1)
    bias = jnp.where(lanes(1) < 32, bias, 0.0)

    for step in range(STEPS):
        copies[2 * step].wait()
        spec[...] = dot(fwd[step, 0], both[...]) + dot(fwd[step, 1], both[...])
        spec[:FREQS, 256:384] += bias
        if step == 0:
            spec[FREQS : FREQS + 1, 256:384] += bias

        def body(i, carry, step=step):
            base = pl.multiple_of(i * rows, rows)
            re, im = pl.ds(base, rows), pl.ds(base + FREQS, rows)
            left, right = slice(0, 128), slice(128, 256)
            s = [rolled(spec[part, side]) for side in (left, right) for part in (re, im)]
            left_t, right_t = slice(256, 384), slice(384, 512)
            t = [rolled(spec[part, side]) for side in (left_t, right_t) for part in (re, im)]
            total = [[None] * 4 for _ in range(2)]

            def add(tile, tap, src):
                terms = (tap[0] * src[0], tap[1] * src[1], tap[1] * src[0], tap[0] * src[1])
                for n, term in enumerate(terms):
                    total[tile][n] = term if total[tile][n] is None else total[tile][n] + term

            for j in range(4):
                near = [pick(position, [t[part][(p - j) % 4] for p in range(4)]) for part in (0, 1)]
                far = [pick(position, [t[part][(p - j) % 4] for p in range(4)]) for part in (2, 3)]
                here = position >= j
                shifted = [jnp.where(here, s[part][j], 0.0) for part in (0, 1)]
                mixed = [jnp.where(here, s[part + 2][j], s[part][j]) for part in (0, 1)]
                add(0, near, shifted)
                add(1, near, mixed)
                add(1, far, shifted)
            prods = []
            for rr, ii, ri, ir in total:
                if step == 0:
                    special = jnp.logical_and(first_row, i == 0)
                    pair = (rr - jnp.where(special, 0.0, ii), jnp.where(special, ii, ri + ir))
                else:
                    pair = (rr - ii, ri + ir)
                prods.append(pair)
            for part, dst in enumerate((re, im)):
                p0, p1 = prods[0][part], prods[1][part]
                q0, q1 = pltpu.roll(p0, 32, 1), pltpu.roll(p1, 32, 1)
                prod[dst, left] = p0 + sign * jnp.where(position >= 1, q0, 0.0)
                prod[dst, right] = p1 + sign * jnp.where(position >= 1, q1, q0)
            return carry

        lax.fori_loop(0, FREQS // rows, body, 0, unroll=16)
        whole = prod[...]
        high = whole.astype(bf16)
        low = (whole - high.astype(f32)).astype(bf16)
        copies[2 * step + 1].wait()
        part = dot(back[step, 0], high) + dot(back[step, 1], high) + dot(back[step, 0], low)
        acc[...] = part if step == 0 else acc[...] + part

    for h in range(2):
        for kk in range(2):
            blocks = [
                acc[kk * 256 + r * 64 : kk * 256 + (r + 1) * 64, h * 128 : (h + 1) * 128]
                for r in range(4)
            ]
            for y, block in enumerate(swap_groups(blocks)):
                out_ref[h * 4 + y, kk] = block.astype(bf16)


def gate_kernel(in_ref, own_ref, partner_ref, out_ref):
    core = lax.axis_index("k")
    for h in range(2):
        cols = slice(h * 128, (h + 1) * 128)
        own_cols = pl.ds(pl.multiple_of(core * 256 + h * 128, 128), 128)
        for other, (ref, at) in enumerate(((own_ref, own_cols), (partner_ref, cols))):
            kk = (core + other) % 2
            blocks = swap_groups([in_ref[h * 4 + y, kk].astype(f32) for y in range(4)])
            for r, conv in enumerate(blocks):
                rows = slice(r * 64, (r + 1) * 64)
                out_ref[other, rows, cols] = (ref[rows, at].astype(f32) * conv).astype(bf16)


PIECES = [(dh, dy, p) for dh in (0, 1) for dy in (0, 1, 2, 3) for p in (0, 1)]


def beside(blocks, p):
    return jnp.concatenate([block[p] for block in blocks], axis=1)


def first_kernel(*refs):
    gated, weights, outs = refs[:4], refs[4:12], refs[12:]
    mine_ref, other_ref, rest_mine, rest_other, rhs, sems = outs
    at = {a: lax.axis_index(a) for a in AXES}
    swapped = (at["k"] + at["l"]) % 2
    pairs = []
    for i, (dh, dy, p) in enumerate(PIECES):
        h, y = (at["h"] + dh) % 2, (at["y"] + dy) % 4
        rest = (y + at["l"] // 2) % 2
        x = (2 * h + y // 2 - at["x"] + 4) % 4
        rows = pl.ds(pl.multiple_of(rest * 1024 + x * 256, 256), 256)
        cols = pl.ds(pl.multiple_of(((swapped + p) % 2) * 512, 512), 512)
        pairs.append((weights[i // 2].at[p], rhs.at[rows, cols]))
    for copy in fetch(pairs, sems):
        copy.wait()
    for p in range(2):
        lhs = beside(gated, p)
        for col, ref in enumerate((mine_ref, other_ref)):
            cols = slice(col * 512, (col + 1) * 512)
            ref[p] = jnp.dot(lhs, rhs[:1024, cols], preferred_element_type=f32)
    rest_mine[...] = rhs[1024:, :512]
    rest_other[...] = rhs[1024:, 512:]


def rest_kernel(g0, g1, g2, g3, before, rhs, own_ref, other_ref):
    for p, ref in enumerate((own_ref, other_ref)):
        lhs = beside((g0, g1, g2, g3), p)
        ref[...] = before[p] + jnp.dot(lhs, rhs[...], preferred_element_type=f32)


VMEM = pl.BlockSpec(memory_space=pltpu.VMEM)
ANY = pl.BlockSpec(memory_space=pl.ANY)


def params(limit=48 * MIB, **kw):
    return pltpu.CompilerParams(vmem_limit_bytes=limit, **kw)


def cost(microseconds):
    rate = 1 << 30
    return pl.CostEstimate(flops=int(microseconds * rate), bytes_accessed=0, transcendentals=0)


def pack(key_in, value_in, taps):
    return pl.pallas_call(
        pack_kernel,
        out_shape=jax.ShapeDtypeStruct((2, 4, 2, 2, 64, 128), bf16),
        in_specs=[ANY] * 3,
        out_specs=VMEM,
        scratch_shapes=[
            pltpu.VMEM((256, 512), bf16),
            pltpu.VMEM((256, 512), bf16),
            pltpu.VMEM((256, 512), f32),
            pltpu.SemaphoreType.DMA((3,)),
        ],
        compiler_params=params(LARGE),
        cost_estimate=cost(2),
        name="pack",
    )(key_in, value_in, taps)


def convolve(received, bias):
    fwd, back = transform_tables()
    return pl.pallas_call(
        conv_kernel,
        out_shape=jax.ShapeDtypeStruct((8, 2, 64, 128), bf16),
        in_specs=[VMEM, VMEM, ANY, ANY],
        out_specs=VMEM,
        scratch_shapes=[
            pltpu.VMEM(fwd.shape, bf16),
            pltpu.VMEM(back.shape, bf16),
            pltpu.VMEM((512, 512), bf16),
            pltpu.VMEM((2 * FREQS, 512), f32),
            pltpu.VMEM((2 * FREQS, 256), f32),
            pltpu.VMEM((512, 256), f32),
            pltpu.SemaphoreType.DMA((2 * STEPS,)),
        ],
        compiler_params=params(LARGE),
        cost_estimate=cost(10),
        name="convolve",
    )(received, bias, jnp.asarray(fwd), jnp.asarray(back))


def gate(conv, own, partner):
    return pl.pallas_call(
        gate_kernel,
        out_shape=jax.ShapeDtypeStruct((2, 256, 256), bf16),
        in_specs=[VMEM] * 3,
        out_specs=VMEM,
        compiler_params=params(),
        cost_estimate=cost(40),
        name="gate",
    )(conv, own, partner)


def project_first(gated, weights):
    part = jax.ShapeDtypeStruct((2, 256, 512), f32)
    rest = jax.ShapeDtypeStruct((1024, 512), bf16)
    return pl.pallas_call(
        first_kernel,
        out_shape=[part, part, rest, rest],
        in_specs=[VMEM] * 4 + [ANY] * 8,
        out_specs=[VMEM] * 4,
        scratch_shapes=[pltpu.VMEM((2048, 1024), bf16), pltpu.SemaphoreType.DMA((16,))],
        compiler_params=params(32 * MIB),
        cost_estimate=cost(5),
        name="project_first",
    )(*gated, *weights)


def project_rest(gated, before, rhs):
    half = jax.ShapeDtypeStruct((256, 512), f32)
    return pl.pallas_call(
        rest_kernel,
        out_shape=[half] * 2,
        in_specs=[VMEM] * 6,
        out_specs=[VMEM] * 2,
        compiler_params=params(32 * MIB),
        cost_estimate=cost(3),
        name="project_rest",
    )(*gated, before, rhs)


def shift(v, axis, by):
    n = lax.axis_size(axis)
    return lax.ppermute(v, axis, [(i, (i + by) % n) for i in range(n)])


def around(v, axis):
    return v, shift(v, axis, -1), shift(v, axis, 2), shift(v, axis, 1)


def body(query, key_in, value_in, filter_taps, conv_bias, out_weight):
    core = lax.axis_index("k")
    tie = lax.optimization_barrier
    bias = conv_bias.reshape(1, 512)
    packed = pack(key_in, value_in, filter_taps)
    received = lax.all_to_all(
        packed.reshape(16, 2, 64, 128), SEQ, split_axis=0, concat_axis=0, tiled=True
    )
    other_half = lax.dynamic_slice(query, (0, (1 - core) * 256), (256, 256))
    partner = shift(other_half, "k", 1)

    swaps = []
    for k in range(2):
        for l in range(4):
            to = (k, l) if k == l % 2 else (1 - k, l ^ 1)
            swaps.append((k * 4 + l, to[0] * 4 + to[1]))
    out_weight = lax.ppermute(out_weight, ("k", "l"), swaps)
    keep = lax.dynamic_slice(out_weight, (core * 256, 0), (256, 512))
    give = lax.dynamic_slice(out_weight, ((1 - core) * 256, 0), (256, 512))
    weight = jnp.stack([keep, shift(give, "k", 1)])
    up, down = shift(weight, "y", 1), shift(weight, "y", -1)
    received, partner, weight = tie((received, partner, weight))

    across = shift(weight, "h", 1)
    conv, up, down, weight = tie((convolve(received, bias), up, down, weight))
    two = shift(weight, "y", 2)
    conv = lax.all_to_all(conv, ("h", "y"), split_axis=0, concat_axis=0, tiled=True)
    two_over = shift(across, "y", 2)
    conv, across = tie((conv, across))

    mine = gate(conv, query, partner)
    other = lax.ppermute(mine, "l", [(i, i ^ 2) for i in range(4)])
    two, two_over, across, other, mine = tie((two, two_over, across, other, around(mine, "x")))
    weights = (weight, down, two, up)
    two = two_over
    other = around(other, "x")
    weights += (across, shift(across, "y", -1), two, shift(across, "y", 1))
    half_mine, half_other, rest_mine, rest_other = project_first(mine, weights)
    other, half_mine, rest_mine = tie((other, half_mine, rest_mine))
    own, partner = project_rest(other, half_other, rest_other)
    send = (own + shift(partner, "k", 1)).astype(bf16)
    from_pair = lax.ppermute(send, "l", [(i, i ^ 1) for i in range(4)])
    own, partner = project_rest(other, half_mine, rest_mine)
    total, from_pair = tie((own + shift(partner, "k", 1), from_pair))
    return (total + from_pair.astype(f32)).astype(bf16)


def solution(mesh):
    fine = Mesh(mesh.devices.reshape(2, 4, 2, 4, 4), AXES)
    block = P(SEQ, CHAN)
    return jax.shard_map(
        body,
        mesh=fine,
        in_specs=(block, block, block, block, P(CHAN), block),
        out_specs=block,
        check_vma=False,
    )
```

```python
import functools

import jax
import jax.numpy as jnp
import numpy as np
from jax import lax
from jax.experimental import pallas as pl
from jax.experimental.pallas import tpu as pltpu
from jax.sharding import Mesh
from jax.sharding import PartitionSpec as P

bf16 = jnp.bfloat16
f32 = jnp.float32
AXES = ("h", "y", "k", "x", "l")
SEQ = ("h", "y", "k")
CHAN = ("x", "l")
N = 1024
STEPS = 4
FREQS = 128
MIB = 1 << 20
LARGE = 60 * MIB


def transform_tables():
    k = np.arange(N // 2)[:, None]
    a = np.arange(N // 2)[None, :]
    angle = 2.0 * np.pi * ((k * a) % N) / N
    re, im = np.cos(angle), -np.sin(angle)
    im[0] = 1.0 - 2.0 * (np.arange(N // 2) % 2)
    weight = np.full((N // 2, 1), 2.0 / N)
    weight[0] = 1.0 / N
    forward = np.concatenate([re.reshape(STEPS, FREQS, -1), im.reshape(STEPS, FREQS, -1)], 1)
    back = np.concatenate(
        [(re * weight).reshape(STEPS, FREQS, -1), (im * weight).reshape(STEPS, FREQS, -1)], 1
    ).transpose(0, 2, 1)

    def split(m):
        high = m.astype(np.float32).astype(jnp.bfloat16)
        low = (m - high.astype(np.float64)).astype(np.float32).astype(jnp.bfloat16)
        return np.stack([high, low], 1)

    return split(forward), split(back)


def lanes(rows):
    return lax.broadcasted_iota(jnp.int32, (rows, 128), 1)


def swap_groups(blocks):
    a0, a1, a2, a3 = blocks
    lane = lanes(a0.shape[0])
    low, even = lane < 64, (lane & 32) == 0
    roll = lambda v, n: pltpu.roll(v, n, 1)
    b0, b2 = jnp.where(low, a0, roll(a2, 64)), jnp.where(low, roll(a0, 64), a2)
    b1, b3 = jnp.where(low, a1, roll(a3, 64)), jnp.where(low, roll(a1, 64), a3)
    c0, c1 = jnp.where(even, b0, roll(b1, 32)), jnp.where(even, roll(b0, 96), b1)
    c2, c3 = jnp.where(even, b2, roll(b3, 32)), jnp.where(even, roll(b2, 96), b3)
    return c0, c1, c2, c3


def fetch(pairs, sems):
    copies = [pltpu.make_async_copy(src, dst, sems.at[i]) for i, (src, dst) in enumerate(pairs)]
    for copy in copies:
        copy.start()
    return copies


def pack_kernel(key_hbm, value_hbm, taps_hbm, out_ref, key_ref, value_ref, taps_ref, sems):
    pairs = ((taps_hbm, taps_ref), (key_hbm, key_ref), (value_hbm, value_ref))
    copies = fetch(pairs, sems)

    def scatter(which, read):
        for v in range(4):
            cols = slice(v * 128, (v + 1) * 128)
            blocks = swap_groups([read(slice(r * 64, (r + 1) * 64), cols) for r in range(4)])
            for y, block in enumerate(blocks):
                out_ref[v % 2, y, v // 2, which] = block.astype(bf16)

    copies[0].wait()
    scatter(1, lambda rows, cols: taps_ref[rows, cols])
    copies[1].wait()
    copies[2].wait()
    scatter(0, lambda rows, cols: key_ref[rows, cols].astype(f32) * value_ref[rows, cols].astype(f32))


def pick(position, choices):
    return jnp.where(
        position == 0,
        choices[0],
        jnp.where(position == 1, choices[1], jnp.where(position == 2, choices[2], choices[3])),
    )


def conv_kernel(in_ref, bias_ref, fwd_hbm, back_hbm, *refs):
    out_ref, fwd, back, both, spec, prod, acc, sems = refs
    tables = []
    for i in range(STEPS):
        tables += [(fwd_hbm.at[i], fwd.at[i]), (back_hbm.at[i], back.at[i])]
    copies = fetch(tables, sems)
    for which in range(2):
        for h in range(2):
            for kk in range(2):
                blocks = [in_ref[h * 8 + y * 2 + kk, which].astype(f32) for y in range(4)]
                for r, block in enumerate(swap_groups(blocks)):
                    row, col = kk * 256 + r * 64, which * 256 + h * 128
                    both[row : row + 64, col : col + 128] = block.astype(bf16)

    dot = functools.partial(jnp.dot, preferred_element_type=f32)
    rows = 8
    position = lanes(rows) // 32
    row_id = lax.broadcasted_iota(jnp.int32, (rows, 128), 0)
    sign = (1 - 2 * (row_id & 1)).astype(f32)
    first_row = row_id == 0

    def rolled(v):
        return [v] + [pltpu.roll(v, 32 * i, 1) for i in (1, 2, 3)]

    start = lax.axis_index("k") * 256 + (lax.axis_index("h") * 4 + lax.axis_index("y")) * 32
    tile = pl.multiple_of(start // 128 * 128, 128)
    bias = pltpu.roll(bias_ref[:, pl.ds(tile, 128)], 128 - start % 128, 1)
    bias = jnp.where(lanes(1) < 32, bias, 0.0)

    for step in range(STEPS):
        copies[2 * step].wait()
        spec[...] = dot(fwd[step, 0], both[...]) + dot(fwd[step, 1], both[...])
        spec[:FREQS, 256:384] += bias
        if step == 0:
            spec[FREQS : FREQS + 1, 256:384] += bias

        def body(i, carry, step=step):
            base = pl.multiple_of(i * rows, rows)
            re, im = pl.ds(base, rows), pl.ds(base + FREQS, rows)
            left, right = slice(0, 128), slice(128, 256)
            s = [rolled(spec[part, side]) for side in (left, right) for part in (re, im)]
            left_t, right_t = slice(256, 384), slice(384, 512)
            t = [rolled(spec[part, side]) for side in (left_t, right_t) for part in (re, im)]
            total = [[None] * 4 for _ in range(2)]

            def add(tile, tap, src):
                terms = (tap[0] * src[0], tap[1] * src[1], tap[1] * src[0], tap[0] * src[1])
                for n, term in enumerate(terms):
                    total[tile][n] = term if total[tile][n] is None else total[tile][n] + term

            for j in range(4):
                near = [pick(position, [t[part][(p - j) % 4] for p in range(4)]) for part in (0, 1)]
                far = [pick(position, [t[part][(p - j) % 4] for p in range(4)]) for part in (2, 3)]
                here = position >= j
                shifted = [jnp.where(here, s[part][j], 0.0) for part in (0, 1)]
                mixed = [jnp.where(here, s[part + 2][j], s[part][j]) for part in (0, 1)]
                add(0, near, shifted)
                add(1, near, mixed)
                add(1, far, shifted)
            prods = []
            for rr, ii, ri, ir in total:
                if step == 0:
                    special = jnp.logical_and(first_row, i == 0)
                    pair = (rr - jnp.where(special, 0.0, ii), jnp.where(special, ii, ri + ir))
                else:
                    pair = (rr - ii, ri + ir)
                prods.append(pair)
            for part, dst in enumerate((re, im)):
                p0, p1 = prods[0][part], prods[1][part]
                q0, q1 = pltpu.roll(p0, 32, 1), pltpu.roll(p1, 32, 1)
                prod[dst, left] = p0 + sign * jnp.where(position >= 1, q0, 0.0)
                prod[dst, right] = p1 + sign * jnp.where(position >= 1, q1, q0)
            return carry

        lax.fori_loop(0, FREQS // rows, body, 0, unroll=16)
        whole = prod[...]
        high = whole.astype(bf16)
        low = (whole - high.astype(f32)).astype(bf16)
        copies[2 * step + 1].wait()
        part = dot(back[step, 0], high) + dot(back[step, 1], high) + dot(back[step, 0], low)
        acc[...] = part if step == 0 else acc[...] + part

    for h in range(2):
        for kk in range(2):
            blocks = [
                acc[kk * 256 + r * 64 : kk * 256 + (r + 1) * 64, h * 128 : (h + 1) * 128]
                for r in range(4)
            ]
            for y, block in enumerate(swap_groups(blocks)):
                out_ref[h * 4 + y, kk] = block.astype(bf16)


def gate_kernel(in_ref, own_ref, partner_ref, out_ref):
    core = lax.axis_index("k")
    for h in range(2):
        cols = slice(h * 128, (h + 1) * 128)
        own_cols = pl.ds(pl.multiple_of(core * 256 + h * 128, 128), 128)
        for other, (ref, at) in enumerate(((own_ref, own_cols), (partner_ref, cols))):
            kk = (core + other) % 2
            blocks = swap_groups([in_ref[h * 4 + y, kk].astype(f32) for y in range(4)])
            for r, conv in enumerate(blocks):
                rows = slice(r * 64, (r + 1) * 64)
                out_ref[other, rows, cols] = (ref[rows, at].astype(f32) * conv).astype(bf16)


PIECES = [(dh, dy, p) for dh in (0, 1) for dy in (0, 1, 2, 3) for p in (0, 1)]


def beside(blocks, p):
    return jnp.concatenate([block[p] for block in blocks], axis=1)


def first_kernel(*refs):
    gated, weights, outs = refs[:4], refs[4:12], refs[12:]
    mine_ref, other_ref, rest_mine, rest_other, rhs, sems = outs
    at = {a: lax.axis_index(a) for a in AXES}
    swapped = (at["k"] + at["l"]) % 2
    pairs = []
    for i, (dh, dy, p) in enumerate(PIECES):
        h, y = (at["h"] + dh) % 2, (at["y"] + dy) % 4
        rest = (y + at["l"] // 2) % 2
        x = (2 * h + y // 2 - at["x"] + 4) % 4
        rows = pl.ds(pl.multiple_of(rest * 1024 + x * 256, 256), 256)
        cols = pl.ds(pl.multiple_of(((swapped + p) % 2) * 512, 512), 512)
        pairs.append((weights[i // 2].at[p], rhs.at[rows, cols]))
    for copy in fetch(pairs, sems):
        copy.wait()
    for p in range(2):
        lhs = beside(gated, p)
        for col, ref in enumerate((mine_ref, other_ref)):
            cols = slice(col * 512, (col + 1) * 512)
            ref[p] = jnp.dot(lhs, rhs[:1024, cols], preferred_element_type=f32)
    rest_mine[...] = rhs[1024:, :512]
    rest_other[...] = rhs[1024:, 512:]


def rest_kernel(g0, g1, g2, g3, before, rhs, own_ref, other_ref):
    for p, ref in enumerate((own_ref, other_ref)):
        lhs = beside((g0, g1, g2, g3), p)
        ref[...] = before[p] + jnp.dot(lhs, rhs[...], preferred_element_type=f32)


VMEM = pl.BlockSpec(memory_space=pltpu.VMEM)
ANY = pl.BlockSpec(memory_space=pl.ANY)


def params(limit=48 * MIB, **kw):
    return pltpu.CompilerParams(vmem_limit_bytes=limit, **kw)


def cost(microseconds):
    rate = 1 << 30
    return pl.CostEstimate(flops=int(microseconds * rate), bytes_accessed=0, transcendentals=0)


def pack(key_in, value_in, taps):
    return pl.pallas_call(
        pack_kernel,
        out_shape=jax.ShapeDtypeStruct((2, 4, 2, 2, 64, 128), bf16),
        in_specs=[ANY] * 3,
        out_specs=VMEM,
        scratch_shapes=[
            pltpu.VMEM((256, 512), bf16),
            pltpu.VMEM((256, 512), bf16),
            pltpu.VMEM((256, 512), f32),
            pltpu.SemaphoreType.DMA((3,)),
        ],
        compiler_params=params(LARGE),
        cost_estimate=cost(2),
        name="pack",
    )(key_in, value_in, taps)


def convolve(received, bias):
    fwd, back = transform_tables()
    return pl.pallas_call(
        conv_kernel,
        out_shape=jax.ShapeDtypeStruct((8, 2, 64, 128), bf16),
        in_specs=[VMEM, VMEM, ANY, ANY],
        out_specs=VMEM,
        scratch_shapes=[
            pltpu.VMEM(fwd.shape, bf16),
            pltpu.VMEM(back.shape, bf16),
            pltpu.VMEM((512, 512), bf16),
            pltpu.VMEM((2 * FREQS, 512), f32),
            pltpu.VMEM((2 * FREQS, 256), f32),
            pltpu.VMEM((512, 256), f32),
            pltpu.SemaphoreType.DMA((2 * STEPS,)),
        ],
        compiler_params=params(LARGE),
        cost_estimate=cost(10),
        name="convolve",
    )(received, bias, jnp.asarray(fwd), jnp.asarray(back))


def gate(conv, own, partner):
    return pl.pallas_call(
        gate_kernel,
        out_shape=jax.ShapeDtypeStruct((2, 256, 256), bf16),
        in_specs=[VMEM] * 3,
        out_specs=VMEM,
        compiler_params=params(),
        cost_estimate=cost(40),
        name="gate",
    )(conv, own, partner)


def project_first(gated, weights):
    part = jax.ShapeDtypeStruct((2, 256, 512), f32)
    rest = jax.ShapeDtypeStruct((1024, 512), bf16)
    return pl.pallas_call(
        first_kernel,
        out_shape=[part, part, rest, rest],
        in_specs=[VMEM] * 4 + [ANY] * 8,
        out_specs=[VMEM] * 4,
        scratch_shapes=[pltpu.VMEM((2048, 1024), bf16), pltpu.SemaphoreType.DMA((16,))],
        compiler_params=params(32 * MIB),
        cost_estimate=cost(5),
        name="project_first",
    )(*gated, *weights)


def project_rest(gated, before, rhs):
    half = jax.ShapeDtypeStruct((256, 512), f32)
    return pl.pallas_call(
        rest_kernel,
        out_shape=[half] * 2,
        in_specs=[VMEM] * 6,
        out_specs=[VMEM] * 2,
        compiler_params=params(32 * MIB),
        cost_estimate=cost(3),
        name="project_rest",
    )(*gated, before, rhs)


def shift(v, axis, by):
    n = lax.axis_size(axis)
    return lax.ppermute(v, axis, [(i, (i + by) % n) for i in range(n)])


def around(v, axis):
    return v, shift(v, axis, -1), shift(v, axis, 2), shift(v, axis, 1)


def body(query, key_in, value_in, filter_taps, conv_bias, out_weight):
    core = lax.axis_index("k")
    tie = lax.optimization_barrier
    bias = conv_bias.reshape(1, 512)
    packed = pack(key_in, value_in, filter_taps)
    received = lax.all_to_all(
        packed.reshape(16, 2, 64, 128), SEQ, split_axis=0, concat_axis=0, tiled=True
    )
    other_half = lax.dynamic_slice(query, (0, (1 - core) * 256), (256, 256))
    partner = shift(other_half, "k", 1)

    swaps = []
    for k in range(2):
        for l in range(4):
            to = (k, l) if k == l % 2 else (1 - k, l ^ 1)
            swaps.append((k * 4 + l, to[0] * 4 + to[1]))
    out_weight = lax.ppermute(out_weight, ("k", "l"), swaps)
    keep = lax.dynamic_slice(out_weight, (core * 256, 0), (256, 512))
    give = lax.dynamic_slice(out_weight, ((1 - core) * 256, 0), (256, 512))
    weight = jnp.stack([keep, shift(give, "k", 1)])
    up, down = shift(weight, "y", 1), shift(weight, "y", -1)
    received, partner, weight = tie((received, partner, weight))

    across = shift(weight, "h", 1)
    conv, up, down, weight = tie((convolve(received, bias), up, down, weight))
    two = shift(weight, "y", 2)
    conv = lax.all_to_all(conv, ("h", "y"), split_axis=0, concat_axis=0, tiled=True)
    two_over = shift(across, "y", 2)
    conv, across = tie((conv, across))

    mine = gate(conv, query, partner)
    other = lax.ppermute(mine, "l", [(i, i ^ 2) for i in range(4)])
    two, across, other, mine = tie((two, across, other, around(mine, "x")))
    weights = (weight, down, two, up)
    two = two_over
    other = around(other, "x")
    weights += (across, shift(across, "y", -1), two, shift(across, "y", 1))
    half_mine, half_other, rest_mine, rest_other = project_first(mine, weights)
    other, half_mine, rest_mine = tie((other, half_mine, rest_mine))
    own, partner = project_rest(other, half_other, rest_other)
    send = (own + shift(partner, "k", 1)).astype(bf16)
    from_pair = lax.ppermute(send, "l", [(i, i ^ 1) for i in range(4)])
    own, partner = project_rest(other, half_mine, rest_mine)
    total, from_pair = tie((own + shift(partner, "k", 1), from_pair))
    return (total + from_pair.astype(f32)).astype(bf16)


def solution(mesh):
    fine = Mesh(mesh.devices.reshape(2, 4, 2, 4, 4), AXES)
    block = P(SEQ, CHAN)
    return jax.shard_map(
        body,
        mesh=fine,
        in_specs=(block, block, block, block, P(CHAN), block),
        out_specs=block,
        check_vma=False,
    )
```

```python
import functools

import jax
import jax.numpy as jnp
import numpy as np
from jax import lax
from jax.experimental import pallas as pl
from jax.experimental.pallas import tpu as pltpu
from jax.sharding import Mesh
from jax.sharding import PartitionSpec as P

bf16 = jnp.bfloat16
f32 = jnp.float32
AXES = ("h", "y", "k", "x", "l")
SEQ = ("h", "y", "k")
CHAN = ("x", "l")
N = 1024
STEPS = 2
FREQS = 256
MIB = 1 << 20
LARGE = 60 * MIB


def transform_tables():
    k = np.arange(N // 2)[:, None]
    a = np.arange(N // 2)[None, :]
    angle = 2.0 * np.pi * ((k * a) % N) / N
    re, im = np.cos(angle), -np.sin(angle)
    im[0] = 1.0 - 2.0 * (np.arange(N // 2) % 2)
    weight = np.full((N // 2, 1), 2.0 / N)
    weight[0] = 1.0 / N
    forward = np.concatenate([re.reshape(STEPS, FREQS, -1), im.reshape(STEPS, FREQS, -1)], 1)
    back = np.concatenate(
        [(re * weight).reshape(STEPS, FREQS, -1), (im * weight).reshape(STEPS, FREQS, -1)], 1
    ).transpose(0, 2, 1)

    def split(m):
        high = m.astype(np.float32).astype(jnp.bfloat16)
        low = (m - high.astype(np.float64)).astype(np.float32).astype(jnp.bfloat16)
        return np.stack([high, low], 1)

    return split(forward), split(back)


def lanes(rows):
    return lax.broadcasted_iota(jnp.int32, (rows, 128), 1)


def swap_groups(blocks):
    a0, a1, a2, a3 = blocks
    lane = lanes(a0.shape[0])
    low, even = lane < 64, (lane & 32) == 0
    roll = lambda v, n: pltpu.roll(v, n, 1)
    b0, b2 = jnp.where(low, a0, roll(a2, 64)), jnp.where(low, roll(a0, 64), a2)
    b1, b3 = jnp.where(low, a1, roll(a3, 64)), jnp.where(low, roll(a1, 64), a3)
    c0, c1 = jnp.where(even, b0, roll(b1, 32)), jnp.where(even, roll(b0, 96), b1)
    c2, c3 = jnp.where(even, b2, roll(b3, 32)), jnp.where(even, roll(b2, 96), b3)
    return c0, c1, c2, c3


def fetch(pairs, sems):
    copies = [pltpu.make_async_copy(src, dst, sems.at[i]) for i, (src, dst) in enumerate(pairs)]
    for copy in copies:
        copy.start()
    return copies


def pack_kernel(key_hbm, value_hbm, taps_hbm, out_ref, key_ref, value_ref, taps_ref, sems):
    pairs = ((taps_hbm, taps_ref), (key_hbm, key_ref), (value_hbm, value_ref))
    copies = fetch(pairs, sems)

    def scatter(which, read):
        for v in range(4):
            cols = slice(v * 128, (v + 1) * 128)
            blocks = swap_groups([read(slice(r * 64, (r + 1) * 64), cols) for r in range(4)])
            for y, block in enumerate(blocks):
                out_ref[v % 2, y, v // 2, which] = block.astype(bf16)

    copies[0].wait()
    scatter(1, lambda rows, cols: taps_ref[rows, cols])
    copies[1].wait()
    copies[2].wait()
    scatter(0, lambda rows, cols: key_ref[rows, cols].astype(f32) * value_ref[rows, cols].astype(f32))


def pick(position, choices):
    return jnp.where(
        position == 0,
        choices[0],
        jnp.where(position == 1, choices[1], jnp.where(position == 2, choices[2], choices[3])),
    )


def conv_kernel(in_ref, bias_ref, fwd_hbm, back_hbm, *refs):
    out_ref, fwd, back, both, spec, prod, acc, sems = refs
    tables = []
    for i in range(STEPS):
        tables += [(fwd_hbm.at[i], fwd.at[i]), (back_hbm.at[i], back.at[i])]
    copies = fetch(tables, sems)
    for which in range(2):
        for h in range(2):
            for kk in range(2):
                blocks = [in_ref[h * 8 + y * 2 + kk, which].astype(f32) for y in range(4)]
                for r, block in enumerate(swap_groups(blocks)):
                    row, col = kk * 256 + r * 64, which * 256 + h * 128
                    both[row : row + 64, col : col + 128] = block.astype(bf16)

    dot = functools.partial(jnp.dot, preferred_element_type=f32)
    rows = 8
    position = lanes(rows) // 32
    row_id = lax.broadcasted_iota(jnp.int32, (rows, 128), 0)
    sign = (1 - 2 * (row_id & 1)).astype(f32)
    first_row = row_id == 0

    def rolled(v):
        return [v] + [pltpu.roll(v, 32 * i, 1) for i in (1, 2, 3)]

    start = lax.axis_index("k") * 256 + (lax.axis_index("h") * 4 + lax.axis_index("y")) * 32
    tile = pl.multiple_of(start // 128 * 128, 128)
    bias = pltpu.roll(bias_ref[:, pl.ds(tile, 128)], 128 - start % 128, 1)
    bias = jnp.where(lanes(1) < 32, bias, 0.0)

    for step in range(STEPS):
        copies[2 * step].wait()
        pair = dot(fwd[step].reshape(4 * FREQS, 512), both[...])
        spec[...] = pair[: 2 * FREQS] + pair[2 * FREQS :]
        spec[:FREQS, 256:384] += bias
        if step == 0:
            spec[FREQS : FREQS + 1, 256:384] += bias

        def body(i, carry, step=step):
            base = pl.multiple_of(i * rows, rows)
            re, im = pl.ds(base, rows), pl.ds(base + FREQS, rows)
            left, right = slice(0, 128), slice(128, 256)
            s = [rolled(spec[part, side]) for side in (left, right) for part in (re, im)]
            left_t, right_t = slice(256, 384), slice(384, 512)
            t = [rolled(spec[part, side]) for side in (left_t, right_t) for part in (re, im)]
            total = [[None] * 4 for _ in range(2)]

            def add(tile, tap, src):
                terms = (tap[0] * src[0], tap[1] * src[1], tap[1] * src[0], tap[0] * src[1])
                for n, term in enumerate(terms):
                    total[tile][n] = term if total[tile][n] is None else total[tile][n] + term

            for j in range(4):
                near = [pick(position, [t[part][(p - j) % 4] for p in range(4)]) for part in (0, 1)]
                far = [pick(position, [t[part][(p - j) % 4] for p in range(4)]) for part in (2, 3)]
                here = position >= j
                shifted = [jnp.where(here, s[part][j], 0.0) for part in (0, 1)]
                mixed = [jnp.where(here, s[part + 2][j], s[part][j]) for part in (0, 1)]
                add(0, near, shifted)
                add(1, near, mixed)
                add(1, far, shifted)
            prods = []
            for rr, ii, ri, ir in total:
                if step == 0:
                    special = jnp.logical_and(first_row, i == 0)
                    pair = (rr - jnp.where(special, 0.0, ii), jnp.where(special, ii, ri + ir))
                else:
                    pair = (rr - ii, ri + ir)
                prods.append(pair)
            for part, dst in enumerate((re, im)):
                p0, p1 = prods[0][part], prods[1][part]
                q0, q1 = pltpu.roll(p0, 32, 1), pltpu.roll(p1, 32, 1)
                prod[dst, left] = p0 + sign * jnp.where(position >= 1, q0, 0.0)
                prod[dst, right] = p1 + sign * jnp.where(position >= 1, q1, q0)
            return carry

        lax.fori_loop(0, FREQS // rows, body, 0, unroll=32)
        whole = prod[...]
        high = whole.astype(bf16)
        low = (whole - high.astype(f32)).astype(bf16)
        copies[2 * step + 1].wait()
        part = dot(back[step, 0], high) + dot(back[step, 1], high) + dot(back[step, 0], low)
        acc[...] = part if step == 0 else acc[...] + part

    for h in range(2):
        for kk in range(2):
            blocks = [
                acc[kk * 256 + r * 64 : kk * 256 + (r + 1) * 64, h * 128 : (h + 1) * 128]
                for r in range(4)
            ]
            for y, block in enumerate(swap_groups(blocks)):
                out_ref[h * 4 + y, kk] = block.astype(bf16)


def gate_kernel(in_ref, own_ref, partner_ref, out_ref):
    core = lax.axis_index("k")
    for h in range(2):
        cols = slice(h * 128, (h + 1) * 128)
        own_cols = pl.ds(pl.multiple_of(core * 256 + h * 128, 128), 128)
        for other, (ref, at) in enumerate(((own_ref, own_cols), (partner_ref, cols))):
            kk = (core + other) % 2
            blocks = swap_groups([in_ref[h * 4 + y, kk].astype(f32) for y in range(4)])
            for r, conv in enumerate(blocks):
                rows = slice(r * 64, (r + 1) * 64)
                out_ref[other, rows, cols] = (ref[rows, at].astype(f32) * conv).astype(bf16)


PIECES = [(dh, dy, p) for dh in (0, 1) for dy in (0, 1, 2, 3) for p in (0, 1)]


def beside(blocks, p):
    return jnp.concatenate([block[p] for block in blocks], axis=1)


def first_kernel(*refs):
    gated, weights, outs = refs[:4], refs[4:12], refs[12:]
    mine_ref, other_ref, rest_mine, rest_other, rhs, sems = outs
    at = {a: lax.axis_index(a) for a in AXES}
    swapped = (at["k"] + at["l"]) % 2
    pairs = []
    for i, (dh, dy, p) in enumerate(PIECES):
        h, y = (at["h"] + dh) % 2, (at["y"] + dy) % 4
        rest = (y + at["l"] // 2) % 2
        x = (2 * h + y // 2 - at["x"] + 4) % 4
        rows = pl.ds(pl.multiple_of(rest * 1024 + x * 256, 256), 256)
        cols = pl.ds(pl.multiple_of(((swapped + p) % 2) * 512, 512), 512)
        pairs.append((weights[i // 2].at[p], rhs.at[rows, cols]))
    for copy in fetch(pairs, sems):
        copy.wait()
    for p in range(2):
        lhs = beside(gated, p)
        for col, ref in enumerate((mine_ref, other_ref)):
            cols = slice(col * 512, (col + 1) * 512)
            ref[p] = jnp.dot(lhs, rhs[:1024, cols], preferred_element_type=f32)
    rest_mine[...] = rhs[1024:, :512]
    rest_other[...] = rhs[1024:, 512:]


def rest_kernel(g0, g1, g2, g3, before, rhs, own_ref, other_ref):
    for p, ref in enumerate((own_ref, other_ref)):
        lhs = beside((g0, g1, g2, g3), p)
        ref[...] = before[p] + jnp.dot(lhs, rhs[...], preferred_element_type=f32)


VMEM = pl.BlockSpec(memory_space=pltpu.VMEM)
ANY = pl.BlockSpec(memory_space=pl.ANY)


def params(limit=48 * MIB, **kw):
    return pltpu.CompilerParams(vmem_limit_bytes=limit, **kw)


def cost(microseconds):
    rate = 1 << 30
    return pl.CostEstimate(flops=int(microseconds * rate), bytes_accessed=0, transcendentals=0)


def pack(key_in, value_in, taps):
    return pl.pallas_call(
        pack_kernel,
        out_shape=jax.ShapeDtypeStruct((2, 4, 2, 2, 64, 128), bf16),
        in_specs=[ANY] * 3,
        out_specs=VMEM,
        scratch_shapes=[
            pltpu.VMEM((256, 512), bf16),
            pltpu.VMEM((256, 512), bf16),
            pltpu.VMEM((256, 512), f32),
            pltpu.SemaphoreType.DMA((3,)),
        ],
        compiler_params=params(LARGE),
        cost_estimate=cost(2),
        name="pack",
    )(key_in, value_in, taps)


def convolve(received, bias):
    fwd, back = transform_tables()
    return pl.pallas_call(
        conv_kernel,
        out_shape=jax.ShapeDtypeStruct((8, 2, 64, 128), bf16),
        in_specs=[VMEM, VMEM, ANY, ANY],
        out_specs=VMEM,
        scratch_shapes=[
            pltpu.VMEM(fwd.shape, bf16),
            pltpu.VMEM(back.shape, bf16),
            pltpu.VMEM((512, 512), bf16),
            pltpu.VMEM((2 * FREQS, 512), f32),
            pltpu.VMEM((2 * FREQS, 256), f32),
            pltpu.VMEM((512, 256), f32),
            pltpu.SemaphoreType.DMA((2 * STEPS,)),
        ],
        compiler_params=params(LARGE),
        cost_estimate=cost(10),
        name="convolve",
    )(received, bias, jnp.asarray(fwd), jnp.asarray(back))


def gate(conv, own, partner):
    return pl.pallas_call(
        gate_kernel,
        out_shape=jax.ShapeDtypeStruct((2, 256, 256), bf16),
        in_specs=[VMEM] * 3,
        out_specs=VMEM,
        compiler_params=params(),
        cost_estimate=cost(40),
        name="gate",
    )(conv, own, partner)


def project_first(gated, weights):
    part = jax.ShapeDtypeStruct((2, 256, 512), f32)
    rest = jax.ShapeDtypeStruct((1024, 512), bf16)
    return pl.pallas_call(
        first_kernel,
        out_shape=[part, part, rest, rest],
        in_specs=[VMEM] * 4 + [ANY] * 8,
        out_specs=[VMEM] * 4,
        scratch_shapes=[pltpu.VMEM((2048, 1024), bf16), pltpu.SemaphoreType.DMA((16,))],
        compiler_params=params(32 * MIB),
        cost_estimate=cost(5),
        name="project_first",
    )(*gated, *weights)


def project_rest(gated, before, rhs):
    half = jax.ShapeDtypeStruct((256, 512), f32)
    return pl.pallas_call(
        rest_kernel,
        out_shape=[half] * 2,
        in_specs=[VMEM] * 6,
        out_specs=[VMEM] * 2,
        compiler_params=params(32 * MIB),
        cost_estimate=cost(3),
        name="project_rest",
    )(*gated, before, rhs)


def shift(v, axis, by):
    n = lax.axis_size(axis)
    return lax.ppermute(v, axis, [(i, (i + by) % n) for i in range(n)])


def around(v, axis):
    return v, shift(v, axis, -1), shift(v, axis, 2), shift(v, axis, 1)


def body(query, key_in, value_in, filter_taps, conv_bias, out_weight):
    core = lax.axis_index("k")
    tie = lax.optimization_barrier
    bias = conv_bias.reshape(1, 512)
    packed = pack(key_in, value_in, filter_taps)
    received = lax.all_to_all(
        packed.reshape(16, 2, 64, 128), SEQ, split_axis=0, concat_axis=0, tiled=True
    )
    other_half = lax.dynamic_slice(query, (0, (1 - core) * 256), (256, 256))
    partner = shift(other_half, "k", 1)

    swaps = []
    for k in range(2):
        for l in range(4):
            to = (k, l) if k == l % 2 else (1 - k, l ^ 1)
            swaps.append((k * 4 + l, to[0] * 4 + to[1]))
    out_weight = lax.ppermute(out_weight, ("k", "l"), swaps)
    keep = lax.dynamic_slice(out_weight, (core * 256, 0), (256, 512))
    give = lax.dynamic_slice(out_weight, ((1 - core) * 256, 0), (256, 512))
    weight = jnp.stack([keep, shift(give, "k", 1)])
    up, down = shift(weight, "y", 1), shift(weight, "y", -1)
    received, partner, weight = tie((received, partner, weight))

    across = shift(weight, "h", 1)
    conv, up, down, weight = tie((convolve(received, bias), up, down, weight))
    two = shift(weight, "y", 2)
    conv = lax.all_to_all(conv, ("h", "y"), split_axis=0, concat_axis=0, tiled=True)
    two_over = shift(across, "y", 2)
    conv, across = tie((conv, across))

    mine = gate(conv, query, partner)
    other = lax.ppermute(mine, "l", [(i, i ^ 2) for i in range(4)])
    two, across, other, mine = tie((two, across, other, around(mine, "x")))
    weights = (weight, down, two, up)
    two = two_over
    other = around(other, "x")
    weights += (across, shift(across, "y", -1), two, shift(across, "y", 1))
    half_mine, half_other, rest_mine, rest_other = project_first(mine, weights)
    other, half_mine, rest_mine = tie((other, half_mine, rest_mine))
    own, partner = project_rest(other, half_other, rest_other)
    send = (own + shift(partner, "k", 1)).astype(bf16)
    from_pair = lax.ppermute(send, "l", [(i, i ^ 1) for i in range(4)])
    own, partner = project_rest(other, half_mine, rest_mine)
    total, from_pair = tie((own + shift(partner, "k", 1), from_pair))
    return (total + from_pair.astype(f32)).astype(bf16)


def solution(mesh):
    fine = Mesh(mesh.devices.reshape(2, 4, 2, 4, 4), AXES)
    block = P(SEQ, CHAN)
    return jax.shard_map(
        body,
        mesh=fine,
        in_specs=(block, block, block, block, P(CHAN), block),
        out_specs=block,
        check_vma=False,
    )
```
